128 devices in a mesh: row: 32 (over z, x_lo, y), col: 4 (over x_hi, core).
Axes of the slice: x: 4 (x_hi: 2, x_lo: 2; x = x_hi * 2 + x_lo), y: 4, z: 4, core: 2. Of those that a mesh axis runs over, the one named last changes fastest.
Arguments:
- text_hidden: bfloat16 [768, 256, 1024], P(('row', 'col')), may hold values from -8 to 8
- lengths: int32 [768], P(('row', 'col')), may hold values from 32 to 256, as said below
- up_weight: bfloat16 [4096, 1024], P(('row', 'col')), may hold values from -0.1875 to 0.1875
- up_bias: bfloat16 [4096], P(('row', 'col')), may hold values from -2 to 2
- down_weight: bfloat16 [4096, 1024], P(('row', 'col')), may hold values from -0.125 to 0.125
- ln_gain: float32 [1024], replicated, may hold values from 0.1 to 1.9
- proj_weight: bfloat16 [1024, 256], replicated, may hold values from -0.1875 to 0.1875
- graph_emb: float32 [768, 256], P('row'), may hold values from -6 to 6
- perm: int32 [768], replicated, may hold values from 0 to 767, each once
Outputs:
- loss: float32 [], replicated
- grad_graph: float32 [768, 256], P('row')
- grad_text: float32 [768, 256], P(('row', 'col'))
- grad_proj: float32 [1024, 256], P(('row', 'col'))
The draws below stay inside these ranges and needn't reach their ends.
Inputs may be any that keep to these rules, and one draw needn't show every extreme that they name: `lengths`: number of valid tokens of each description; the first description is full.
All inputs are finite; a program needn't handle non-finite values.
Results may differ from the reference program's by a relative error of at most 0.0056.
Values may be sent and summed in bfloat16 or wider, within the bound.
No kernel may reach another device: no remote copies, remote signals or barrier semaphores. Data moves between devices by JAX's collectives and lax.ppermute only.
A program may use at most 128 MiB of HBM per device.

```python
import jax
import jax.numpy as jnp
from jax import lax

D = 1024
FF = 4096
E = 256
L = 256
B = 768


def draw_lengths(key, part):
    key = jax.random.fold_in(key, 7)
    values = jax.random.randint(key, (B,), L // 8, L + 1, dtype=jnp.int32)
    return values.at[0].set(L)


def draw_text_hidden(key, part):
    key = jax.random.fold_in(key, 11)
    noise_key, offset_key = jax.random.split(key, 2)
    noise = jax.random.normal(noise_key, (B, L, D), jnp.float32)
    offset = jax.random.normal(offset_key, (B, 1, D), jnp.float32)
    values = noise + 1.5 * offset
    return jnp.clip(values, -8.0, 8.0).astype(jnp.bfloat16)


def block_scale(rng, shape, pieces, least, largest):
    def one(position, shards_of):
        steps = jax.random.uniform(jax.random.fold_in(jax.random.fold_in(rng, 6), position), (shards_of,), jnp.float32, least / len(pieces), largest / len(pieces))
        return jnp.repeat(jnp.exp(steps), shape[position] // shards_of).reshape((-1,) + (1,) * (len(shape) - position - 1))

    loudness = one(*pieces[0])
    for cut in pieces[1:]:
        loudness = loudness * one(*cut)
    return loudness


def normal_values(rng, shape, scale, most, pieces=(), kind=jnp.bfloat16):
    entries = scale * jax.random.normal(rng, shape, jnp.float32)
    if pieces:
        entries = entries * block_scale(rng, shape, pieces, -0.22, 0.18)
    return jnp.clip(entries, -most, most).astype(kind)


def setup_inputs(seed: int = 0) -> dict:
    keys = jax.random.split(jax.random.key(seed), 10)
    return {
        "text_hidden": draw_text_hidden(jax.random.fold_in(keys[9], 71), 0),
        "lengths": draw_lengths(jax.random.fold_in(keys[9], 71), 0),
        "up_weight": normal_values(keys[2], (FF, D), D ** -0.5, 0.1875, ((0, 128),)),
        "up_bias": normal_values(keys[3], (FF,), 0.5, 2.0, ((0, 128),)),
        "down_weight": normal_values(keys[4], (FF, D), (FF // 2) ** -0.5, 0.125, ((0, 128),)),
        "ln_gain": jnp.clip(1.0 + 0.18 * jax.random.normal(keys[5], (D,), jnp.float32), 0.1, 1.9),
        "proj_weight": normal_values(keys[6], (D, E), D ** -0.5, 0.1875),
        "graph_emb": normal_values(keys[7], (B, E), 1.0, 6.0, ((0, 32),), jnp.float32),
        "perm": jax.random.permutation(keys[8], B).astype(jnp.int32),
    }


sharpness_divisor = 0.02
epsilon = 1e-06

def hidden_block(tokens_in, weight_in, bias_in, weight_out):
    preact = lax.dot_general(tokens_in, weight_in, (((1,), (1,)), ((), ())), preferred_element_type=jnp.float32) + bias_in.astype(jnp.float32)
    active = jax.nn.gelu(preact, approximate=False).astype(jnp.bfloat16)
    return jnp.dot(active, weight_out, preferred_element_type=jnp.float32)

def norm_pool(tokens_in, ffn_out, ln_gain, lengths, seq_count, seq_len):
    summed = tokens_in.astype(jnp.float32) + ffn_out
    centre = summed - lax.optimization_barrier(jnp.mean(summed, axis=-1, keepdims=True))
    spread = lax.optimization_barrier(jnp.mean(centre * centre, axis=-1, keepdims=True))
    normed = centre * lax.rsqrt(spread + epsilon) * ln_gain
    normed = normed.reshape(seq_count, seq_len, -1)
    valid = (jnp.arange(seq_len, dtype=jnp.int32)[None, :] < lengths[:, None]).astype(jnp.float32)
    return lax.optimization_barrier(jnp.sum(normed * valid[:, :, None], axis=1)) / lengths[:, None].astype(jnp.float32)

def unit_rows(values):
    norm_rows = jnp.sqrt(lax.optimization_barrier(jnp.sum(values * values, axis=-1, keepdims=True)) + epsilon)
    return (values / norm_rows, norm_rows)

def reference(text_hidden, lengths, up_weight, up_bias, down_weight, ln_gain, proj_weight, graph_emb, perm):

    def one_sequence(packed):
        sequence, valid_count = packed
        ffn_out = hidden_block(sequence, up_weight, up_bias, down_weight)
        return norm_pool(sequence, ffn_out, ln_gain, valid_count[None], 1, L)[0]
    pooled = lax.map(one_sequence, (text_hidden, lengths)).astype(jnp.bfloat16)
    text_emb = jnp.dot(pooled, proj_weight, preferred_element_type=jnp.float32)
    text_unit, text_norm = unit_rows(text_emb)
    graph_unit, graph_norm = unit_rows(graph_emb)
    text_send = text_unit.astype(jnp.bfloat16)
    molecule_dispatched = graph_unit.astype(jnp.bfloat16)
    caption_mesh = jnp.zeros_like(text_send).at[perm].set(text_send)
    pairwise_scores = jnp.dot(molecule_dispatched, caption_mesh.T, preferred_element_type=jnp.float32) / sharpness_divisor
    expo = jnp.exp(pairwise_scores)
    row_total = lax.optimization_barrier(jnp.sum(expo, axis=1))
    col_total = lax.optimization_barrier(jnp.sum(expo, axis=0))
    diag_sum = jnp.sum(jnp.diagonal(pairwise_scores))
    loss = (jnp.sum(jnp.log(row_total)) + jnp.sum(jnp.log(col_total)) - 2.0 * diag_sum) / (2.0 * B)
    identity = jnp.eye(B, dtype=jnp.float32)
    sublevel_parameters = ((expo / row_total[:, None] + expo / col_total[None, :]) * 0.5 - identity).astype(jnp.bfloat16)
    molecule_derivative_unitized = jnp.dot(sublevel_parameters, caption_mesh, preferred_element_type=jnp.float32) / sharpness_divisor
    caption_derivative_mesh = jnp.dot(sublevel_parameters.T, molecule_dispatched, preferred_element_type=jnp.float32) / sharpness_divisor
    grad_graph = (molecule_derivative_unitized - graph_unit * lax.optimization_barrier(jnp.sum(graph_unit * molecule_derivative_unitized, axis=-1, keepdims=True))) / graph_norm
    caption_derivative_unitized = caption_derivative_mesh[perm]
    grad_text = (caption_derivative_unitized - text_unit * lax.optimization_barrier(jnp.sum(text_unit * caption_derivative_unitized, axis=-1, keepdims=True))) / text_norm
    grad_proj = jnp.dot(pooled.astype(jnp.float32).T, grad_text, precision=lax.Precision.HIGHEST)
    return (loss, grad_graph, grad_text, grad_proj)
```

```python
import functools

import jax
import jax.numpy as jnp
from jax import lax
from jax.experimental import pallas as pl
from jax.experimental.pallas import tpu as pltpu
from jax.sharding import PartitionSpec as P

sharpness_divisor = 0.02
epsilon = 1e-06
axes = ("row", "col")
block_rows = 256
erf_terms = (
    -5.7109417639367166e-08,
    2.812487991832313e-06,
    -4.7398178139701486e-05,
    -5.735534068662673e-05,
    0.03636491671204567,
    0.7978729605674744,
)
nt = (((1,), (1,)), ((), ()))
tn = (((0,), (0,)), ((), ()))


def flat_index(x, y, z, core):
    return (z * 8 + (x % 2) * 4 + y) * 4 + (x // 2) * 2 + core


def pairs(dx=0, dy=0, dz=0, dc=0, by_core=False):
    found = []
    for x in range(4):
        for y in range(4):
            for z in range(4):
                for core in range(2):
                    sign = -1 if by_core and core else 1
                    target = flat_index(
                        (x + sign * dx) % 4, (y + sign * dy) % 4, (z + sign * dz) % 4, core ^ dc
                    )
                    found.append((flat_index(x, y, z, core), target))
    return found


def send(value, **hop):
    return lax.ppermute(value, axes, pairs(**hop))


def from_line(value, axis):
    return [value] + [send(value, **{axis: hop}) for hop in (1, 3, 2)]


def gelu_exact(x):
    square = jnp.minimum(x * x, 25.0)
    series = jnp.full_like(square, erf_terms[0])
    for term in erf_terms[1:]:
        series = series * square + term
    half = 0.5 * x
    return half + half * jnp.tanh(x * series)


def pack_kernel(meta, source, packed, sem):
    for s in range(6):
        start = pl.multiple_of(meta[s], 16)
        copy = pltpu.make_async_copy(source.at[s], packed.at[pl.ds(start, 256)], sem)
        copy.start()
        copy.wait()


def pack_tokens(meta, text_hidden):
    seqs, seq_len, width = text_hidden.shape
    return pl.pallas_call(
        pack_kernel,
        grid_spec=pltpu.PrefetchScalarGridSpec(
            num_scalar_prefetch=1,
            grid=(),
            in_specs=[pl.BlockSpec(memory_space=pl.ANY)],
            out_specs=pl.BlockSpec(memory_space=pl.ANY),
            scratch_shapes=[pltpu.SemaphoreType.DMA],
        ),
        out_shape=jax.ShapeDtypeStruct((seqs * seq_len, width), jnp.bfloat16),
    )(meta, text_hidden)


def ffn_tiles(x, weights):
    total = None
    lane = lax.broadcasted_iota(jnp.int32, (1, 256), 1) // 64
    for first, second in zip(weights[::2], weights[1::2]):
        up = jnp.concatenate([first[0:128, :], second[0:128, :]], axis=0)
        down = jnp.concatenate([first[128:256, :], second[128:256, :]], axis=0)
        b0 = first[256:272, 0:256].astype(jnp.float32)
        b1 = second[256:272, 0:256].astype(jnp.float32)
        bias = jnp.where(
            lane < 2,
            jnp.where(lane == 0, b0[0:1], b0[8:9]),
            jnp.where(lane == 2, b1[0:1], b1[8:9]),
        )
        preact = lax.dot_general(x, up, nt, preferred_element_type=jnp.float32) + bias
        active = gelu_exact(preact).astype(jnp.bfloat16)
        part = jnp.dot(active, down, preferred_element_type=jnp.float32)
        total = part if total is None else total + part
    return total


def ffn_kernel(count, first, last, meta, x_ref, *refs):
    weights = refs[:count]
    refs = refs[count:]
    i = pl.program_id(0)
    live = i < meta[13]
    if not first:
        acc_in, refs = refs[0], refs[1:]
    if not last:
        (out_ref,) = refs

        @pl.when(live)
        def _():
            total = ffn_tiles(x_ref[...], weights)
            out_ref[...] = total if first else acc_in[...] + total

        return
    gain_ref, pooled_ref, sums = refs

    @pl.when(i == 0)
    def _():
        sums[...] = jnp.zeros_like(sums)

    @pl.when(live)
    def _():
        x = x_ref[...]
        summed = x.astype(jnp.float32) + (acc_in[...] + ffn_tiles(x, weights))
        centre = summed - jnp.mean(summed, axis=-1, keepdims=True)
        spread = jnp.mean(centre * centre, axis=-1, keepdims=True)
        normed = centre * lax.rsqrt(spread + epsilon) * gain_ref[...]
        base = i * block_rows
        row = base + lax.broadcasted_iota(jnp.int32, (block_rows, 1), 0)
        normed = jnp.where(row < meta[12], normed, 0.0)
        column = base + lax.broadcasted_iota(jnp.int32, (8, block_rows), 1)
        seq = lax.broadcasted_iota(jnp.int32, (8, block_rows), 0)
        member = jnp.zeros((8, block_rows), jnp.float32)
        for s in range(6):
            inside = (column >= meta[s]) & (column < meta[s] + meta[6 + s]) & (seq == s)
            member = jnp.where(inside, 1.0, member)
        sums[...] += jnp.dot(
            member, normed, precision=lax.Precision.HIGHEST, preferred_element_type=jnp.float32
        )

    @pl.when(i == pl.num_programs(0) - 1)
    def _():
        seq = lax.broadcasted_iota(jnp.int32, (8, 1), 0)
        tokens = jnp.ones((8, 1), jnp.float32)
        for s in range(6):
            tokens = jnp.where(seq == s, meta[6 + s].astype(jnp.float32), tokens)
        pooled_ref[...] = (sums[...] / tokens).astype(jnp.bfloat16)


def ffn_step(meta, packed, weights, acc=None, gain=None):
    rows, width = packed.shape
    count, first, last = len(weights), acc is None, gain is not None
    steps = rows // block_rows
    row_block = pl.BlockSpec((block_rows, width), lambda i, m: (jnp.minimum(i, m[13] - 1), 0))
    whole = lambda shape: pl.BlockSpec(shape, lambda i, m: (0, 0))
    in_specs = [row_block] + [whole(w.shape) for w in weights]
    operands = [packed, *weights]
    if not first:
        in_specs.append(row_block)
        operands.append(acc)
    scratch = []
    if last:
        in_specs.append(whole((1, width)))
        operands.append(gain)
        out_shape = jax.ShapeDtypeStruct((8, width), jnp.bfloat16)
        out_specs = whole((8, width))
        scratch = [pltpu.VMEM((8, width), jnp.float32)]
    else:
        out_shape = jax.ShapeDtypeStruct((rows, width), jnp.float32)
        out_specs = row_block
    hidden = 128 * count
    return pl.pallas_call(
        functools.partial(ffn_kernel, count, first, last),
        grid_spec=pltpu.PrefetchScalarGridSpec(
            num_scalar_prefetch=1,
            grid=(steps,),
            in_specs=in_specs,
            out_specs=out_specs,
            scratch_shapes=scratch,
        ),
        out_shape=out_shape,
        compiler_params=pltpu.CompilerParams(
            dimension_semantics=("arbitrary",), vmem_limit_bytes=40 * 2**20
        ),
        cost_estimate=pl.CostEstimate(
            flops=3 * rows * hidden * width, bytes_accessed=10 * 2**20, transcendentals=0
        ),
    )(meta, *operands)


def tail_kernel(
    place,
    pooled_ref,
    proj_ref,
    graph_ref,
    own_ref,
    slot_ref,
    loss_ref,
    grad_graph_ref,
    grad_text_ref,
    grad_proj_ref,
):
    texts = pooled_ref.shape[0]
    graphs = graph_ref.shape[0]
    flat, row_first = place[0], place[1]
    pooled = pooled_ref[...]
    text_emb = jnp.dot(pooled, proj_ref[...], preferred_element_type=jnp.float32)
    text_norm = jnp.sqrt(jnp.sum(text_emb * text_emb, axis=-1, keepdims=True) + epsilon)
    text_unit = text_emb / text_norm
    text_send = text_unit.astype(jnp.bfloat16)
    graph_send = graph_ref[...]
    slot = slot_ref[...]
    valid = slot >= 0

    def scores(rows_send):
        logits = (
            lax.dot_general(rows_send, text_send, nt, preferred_element_type=jnp.float32)
            / sharpness_divisor
        )
        expo = jnp.where(valid, jnp.exp(logits), 0.0)
        return logits, expo, jnp.sum(expo, axis=1, keepdims=True)

    logits, expo, row_total = scores(graph_send)
    col_total = jnp.where(valid, jnp.sum(expo, axis=0, keepdims=True), 1.0)
    col_scale = 0.5 / col_total
    matched = lax.broadcasted_iota(jnp.int32, (graphs, texts), 0) == slot
    diagonal = jnp.sum(jnp.where(matched, logits, 0.0), axis=1, keepdims=True)
    row_terms = jnp.sum(jnp.log(row_total) - 2.0 * diagonal, axis=0, keepdims=True)
    col_terms = jnp.sum(jnp.log(col_total), axis=1, keepdims=True)
    loss_ref[...] = (row_terms + col_terms) / (2.0 * graphs)

    def weigh(expo, row_total, matched):
        weights = expo * (0.5 / row_total) + expo * col_scale
        return (weights - jnp.where(matched, 1.0, 0.0)).astype(jnp.bfloat16)

    weights = weigh(expo, row_total, matched)
    text_grad = (
        lax.dot_general(weights, graph_send, tn, preferred_element_type=jnp.float32)
        / sharpness_divisor
    )
    along = jnp.sum(text_unit * text_grad, axis=-1, keepdims=True)
    grad_text = (text_grad - text_unit * along) / text_norm
    grad_text_ref[...] = grad_text[0:8]

    own = own_ref[...]
    own_norm = jnp.sqrt(jnp.sum(own * own, axis=-1, keepdims=True) + epsilon)
    own_unit = own / own_norm
    _, own_expo, own_total = scores(own_unit.astype(jnp.bfloat16))
    own_rows = own.shape[0]
    own_matched = row_first + lax.broadcasted_iota(jnp.int32, (own_rows, texts), 0) == slot
    own_weights = weigh(own_expo, own_total, own_matched)
    graph_grad = (
        jnp.dot(own_weights, text_send, preferred_element_type=jnp.float32) / sharpness_divisor
    )
    own_along = jnp.sum(own_unit * graph_grad, axis=-1, keepdims=True)
    grad_graph_ref[...] = (graph_grad - own_unit * own_along) / own_norm

    width = pooled.shape[1]
    feature = lax.broadcasted_iota(jnp.int32, (width, 128), 0)
    wanted = flat * 8 + lax.broadcasted_iota(jnp.int32, (width, 128), 1)
    pick = (feature == wanted).astype(jnp.bfloat16)
    picked = jnp.dot(pooled, pick, preferred_element_type=jnp.float32)
    grad_proj = lax.dot_general(
        picked,
        grad_text,
        tn,
        precision=lax.Precision.HIGHEST,
        preferred_element_type=jnp.float32,
    )
    grad_proj_ref[...] = grad_proj[0:8]


def tail(place, pooled_all, proj_weight, graph_all, graph_emb, slot):
    shapes = [(1, 1), graph_emb.shape, (8, 256), (8, 256)]
    return pl.pallas_call(
        tail_kernel,
        in_specs=[pl.BlockSpec(memory_space=pltpu.SMEM)]
        + [pl.BlockSpec(memory_space=pltpu.VMEM)] * 5,
        out_specs=[pl.BlockSpec(memory_space=pltpu.VMEM)] * 4,
        out_shape=[jax.ShapeDtypeStruct(s, jnp.float32) for s in shapes],
        compiler_params=pltpu.CompilerParams(vmem_limit_bytes=48 * 2**20),
    )(place, pooled_all, proj_weight, graph_all, graph_emb, slot)


def gather_weights(up_weight, up_bias, down_weight):
    width = up_weight.shape[1]
    bias_rows = jnp.pad(up_bias.reshape(1, 32), ((0, 7), (0, width - 32)))
    own = jnp.concatenate([up_weight, down_weight, bias_rows], axis=0)
    line = from_line(own, "dz")

    def half(k):
        up = [v[16 * k : 16 * k + 16] for v in line]
        down = [v[32 + 16 * k : 48 + 16 * k] for v in line]
        bias = jnp.concatenate([v[64:65, 16 * k : 16 * k + 16] for v in line], axis=1)
        bias = jnp.pad(jnp.tile(bias, (1, width // 64)), ((0, 7), (0, 0)))
        return jnp.concatenate(up + down + [bias], axis=0)

    def join(a, b):
        return jnp.concatenate(
            [a[0:64], b[0:64], a[64:128], b[64:128], a[128:136], b[128:136]], axis=0
        )

    halves = []
    for k, (inner, outer) in enumerate((("dx", "dy"), ("dy", "dx"))):
        ring = [half(k)]
        for _ in range(3):
            ring.append(send(ring[-1], by_core=True, **{inner: 1}))
        blocks = []
        for start in (join(ring[0], ring[1]), join(ring[2], ring[3])):
            steps = [start]
            for _ in range(3):
                steps.append(send(steps[-1], by_core=True, **{outer: 1}))
            blocks.append(steps)
        halves.append(blocks)
    order = [(0, 0), (0, 1), (1, 0), (0, 2), (1, 1), (0, 3), (1, 2), (1, 3)]
    groups = []
    for at in range(0, 8, 2):
        mine, other = [], []
        for block, step in order[at : at + 2]:
            for k in range(2):
                value = halves[k][block][step]
                mine.append(value)
                other.append(send(value, dc=1))
        groups.append(mine + other)
    return groups


def shards(
    text_hidden, lengths, up_weight, up_bias, down_weight, ln_gain, proj_weight, graph_emb, perm
):
    row_index = lax.axis_index("row")
    col_index = lax.axis_index("col")
    z, y = row_index // 8, row_index % 4
    x = (col_index // 2) * 2 + (row_index // 4) % 2
    core = col_index % 2
    flat = row_index * 4 + col_index

    padded = (lengths + 15) // 16 * 16
    starts = jnp.cumsum(padded) - padded
    total = jnp.sum(padded)
    row_blocks = (total + block_rows - 1) // block_rows
    meta = jnp.concatenate(
        [starts, lengths, jnp.stack([total, row_blocks]), jnp.zeros((2,), jnp.int32)]
    ).astype(jnp.int32)

    packed = pack_tokens(meta, text_hidden)
    groups = gather_weights(up_weight, up_bias, down_weight)
    graph_norm = jnp.sqrt(jnp.sum(graph_emb * graph_emb, axis=-1, keepdims=True) + epsilon)
    graph_send = (graph_emb / graph_norm).astype(jnp.bfloat16)
    graph_all = lax.all_gather(graph_send, "row", axis=0, tiled=True)

    acc = None
    for at, group in enumerate(groups):
        gain = ln_gain.reshape(1, -1) if at == len(groups) - 1 else None
        acc = ffn_step(meta, packed, group, acc, gain)
    pooled = acc
    for axis in ("dz", "dy", "dx"):
        pooled = jnp.concatenate(from_line(pooled, axis), axis=0)
    pooled_all = jnp.concatenate([pooled, send(pooled, dc=1)], axis=0)

    rel = jnp.array([0, -1, 1, 2], jnp.int32)
    ids = flat_index(
        ((x + rel) % 4)[None, :, None, None],
        ((y + rel) % 4)[None, None, :, None],
        ((z + rel) % 4)[None, None, None, :],
        (core ^ jnp.arange(2, dtype=jnp.int32))[:, None, None, None],
    ).reshape(-1, 1)
    lane = jnp.arange(8, dtype=jnp.int32)[None, :]
    tower = jnp.where(lane < 6, ids * 6 + lane, -1).reshape(-1)
    pairs_all = perm.shape[0]
    hit = tower[None, :] == jnp.arange(pairs_all, dtype=jnp.int32)[:, None]
    slot = jnp.sum(jnp.where(hit, perm[:, None] + 1, 0), axis=0, keepdims=True) - 1
    place = jnp.stack([flat, row_index * graph_emb.shape[0]]).astype(jnp.int32)
    loss, grad_graph, grad_text, grad_proj = tail(
        place, pooled_all, proj_weight, graph_all, graph_emb, slot.astype(jnp.int32)
    )
    return (loss[0, 0], grad_graph, grad_text[:6], grad_proj)


def solution(mesh):
    return jax.shard_map(
        shards,
        mesh=mesh,
        in_specs=(
            P(("row", "col"), None, None),
            P(("row", "col")),
            P(("row", "col"), None),
            P(("row", "col")),
            P(("row", "col"), None),
            P(),
            P(),
            P("row", None),
            P(),
        ),
        out_specs=(P(), P("row", None), P(("row", "col"), None), P(("row", "col"), None)),
        check_vma=False,
    )
```

```python
import functools

import jax
import jax.numpy as jnp
from jax import lax
from jax.experimental import pallas as pl
from jax.experimental.pallas import tpu as pltpu
from jax.sharding import PartitionSpec as P

sharpness_divisor = 0.02
epsilon = 1e-06
axes = ("row", "col")
block_rows = 256
erf_terms = (
    -5.7109417639367166e-08,
    2.812487991832313e-06,
    -4.7398178139701486e-05,
    -5.735534068662673e-05,
    0.03636491671204567,
    0.7978729605674744,
)
nt = (((1,), (1,)), ((), ()))
tn = (((0,), (0,)), ((), ()))


def flat_index(x, y, z, core):
    return (z * 8 + (x % 2) * 4 + y) * 4 + (x // 2) * 2 + core


def pairs(dx=0, dy=0, dz=0, dc=0, by_core=False):
    found = []
    for x in range(4):
        for y in range(4):
            for z in range(4):
                for core in range(2):
                    sign = -1 if by_core and core else 1
                    target = flat_index(
                        (x + sign * dx) % 4, (y + sign * dy) % 4, (z + sign * dz) % 4, core ^ dc
                    )
                    found.append((flat_index(x, y, z, core), target))
    return found


def send(value, **hop):
    return lax.ppermute(value, axes, pairs(**hop))


def from_line(value, axis):
    return [value] + [send(value, **{axis: hop}) for hop in (1, 3, 2)]


def gelu_exact(x):
    square = jnp.minimum(x * x, 25.0)
    series = jnp.full_like(square, erf_terms[0])
    for term in erf_terms[1:]:
        series = series * square + term
    half = 0.5 * x
    return half + half * jnp.tanh(x * series)


def pack_kernel(meta, source, packed, sem):
    for s in range(6):
        start = pl.multiple_of(meta[s], 16)
        copy = pltpu.make_async_copy(source.at[s], packed.at[pl.ds(start, 256)], sem)
        copy.start()
        copy.wait()


def pack_tokens(meta, text_hidden):
    seqs, seq_len, width = text_hidden.shape
    return pl.pallas_call(
        pack_kernel,
        grid_spec=pltpu.PrefetchScalarGridSpec(
            num_scalar_prefetch=1,
            grid=(),
            in_specs=[pl.BlockSpec(memory_space=pl.ANY)],
            out_specs=pl.BlockSpec(memory_space=pltpu.VMEM),
            scratch_shapes=[pltpu.SemaphoreType.DMA],
        ),
        out_shape=jax.ShapeDtypeStruct((seqs * seq_len, width), jnp.bfloat16),
        compiler_params=pltpu.CompilerParams(vmem_limit_bytes=16 * 2**20),
    )(meta, text_hidden)


def merge_bias(tiles, run):
    lane = lax.broadcasted_iota(jnp.int32, (1, tiles[0].shape[1]), 1) // run % 4
    row = tiles[0].astype(jnp.float32)[0:1]
    for k in range(1, 4):
        row = jnp.where(lane == k, tiles[k].astype(jnp.float32)[0:1], row)
    return jnp.broadcast_to(row, tiles[0].shape).astype(jnp.bfloat16)


def split_kernel(*refs):
    parts = refs[:4]
    for k, out in enumerate(refs[4:]):
        for s, part in enumerate(parts):
            out[16 * s : 16 * s + 16, :] = part[16 * k : 16 * k + 16, :]
            out[64 + 16 * s : 80 + 16 * s, :] = part[32 + 16 * k : 48 + 16 * k, :]
        out[128:144, :] = merge_bias([p[64 + 16 * k : 80 + 16 * k, :] for p in parts], 16)


def join_kernel(*refs):
    for k, out in enumerate(refs[8:]):
        parts = refs[4 * k : 4 * k + 4]
        for s, part in enumerate(parts):
            out[64 * s : 64 * s + 64, :] = part[0:64, :]
            out[256 + 64 * s : 320 + 64 * s, :] = part[64:128, :]
        out[512:528, :] = merge_bias([p[128:144, :] for p in parts], 64)


def arrange(body, parts, rows):
    shape = jax.ShapeDtypeStruct((rows, parts[0].shape[1]), jnp.bfloat16)
    return pl.pallas_call(
        body,
        in_specs=[pl.BlockSpec(memory_space=pltpu.VMEM)] * len(parts),
        out_specs=[pl.BlockSpec(memory_space=pltpu.VMEM)] * 2,
        out_shape=[shape, shape],
        compiler_params=pltpu.CompilerParams(vmem_limit_bytes=16 * 2**20),
    )(*parts)


def ffn_tiles(x, weights):
    up = jnp.concatenate([w[0:256, :] for w in weights], axis=0)
    down = jnp.concatenate([w[256:512, :] for w in weights], axis=0)
    bias = jnp.concatenate(
        [w[512:528, 0:256].astype(jnp.float32)[0:1] for w in weights], axis=1
    )
    preact = lax.dot_general(x, up, nt, preferred_element_type=jnp.float32) + bias
    active = gelu_exact(preact).astype(jnp.bfloat16)
    return jnp.dot(active, down, preferred_element_type=jnp.float32)


def ffn_kernel(count, first, last, meta, x_ref, *refs):
    weights = refs[:count]
    refs = refs[count:]
    i = pl.program_id(0)
    live = i < meta[13]
    if not first:
        acc_in, refs = refs[0], refs[1:]
    if not last:
        (out_ref,) = refs

        @pl.when(live)
        def _():
            total = ffn_tiles(x_ref[...], weights)
            out_ref[...] = total if first else acc_in[...] + total

        return
    gain_ref, graph_ref, pooled_ref, sums = refs

    @pl.when(i == 0)
    def _():
        sums[...] = jnp.zeros_like(sums)

    @pl.when(live)
    def _():
        x = x_ref[...]
        summed = x.astype(jnp.float32) + (acc_in[...] + ffn_tiles(x, weights))
        centre = summed - jnp.mean(summed, axis=-1, keepdims=True)
        spread = jnp.mean(centre * centre, axis=-1, keepdims=True)
        normed = centre * lax.rsqrt(spread + epsilon) * gain_ref[...]
        base = i * block_rows
        row = base + lax.broadcasted_iota(jnp.int32, (block_rows, 1), 0)
        normed = jnp.where(row < meta[12], normed, 0.0)
        column = base + lax.broadcasted_iota(jnp.int32, (8, block_rows), 1)
        seq = lax.broadcasted_iota(jnp.int32, (8, block_rows), 0)
        member = jnp.zeros((8, block_rows), jnp.float32)
        for s in range(6):
            inside = (column >= meta[s]) & (column < meta[s] + meta[6 + s]) & (seq == s)
            member = jnp.where(inside, 1.0, member)
        sums[...] += jnp.dot(
            member, normed, precision=lax.Precision.HIGHEST, preferred_element_type=jnp.float32
        )

    @pl.when(i == pl.num_programs(0) - 1)
    def _():
        seq = lax.broadcasted_iota(jnp.int32, (8, 1), 0)
        tokens = jnp.ones((8, 1), jnp.float32)
        for s in range(6):
            tokens = jnp.where(seq == s, meta[6 + s].astype(jnp.float32), tokens)
        means = (sums[...] / tokens).astype(jnp.bfloat16)
        pooled_ref[...] = jnp.where(seq < 6, means, graph_ref[...])


def ffn_step(meta, packed, weights, acc=None, gain=None, graph_rows=None):
    rows, width = packed.shape
    count, first, last = len(weights), acc is None, gain is not None
    steps = rows // block_rows
    row_block = pl.BlockSpec((block_rows, width), lambda i, m: (jnp.minimum(i, m[13] - 1), 0))
    whole = lambda shape: pl.BlockSpec(shape, lambda i, m: (0, 0))
    in_specs = [row_block] + [whole(w.shape) for w in weights]
    operands = [packed, *weights]
    if not first:
        in_specs.append(row_block)
        operands.append(acc)
    scratch = []
    if last:
        in_specs += [whole((1, width)), whole((8, width))]
        operands += [gain, graph_rows]
        out_shape = jax.ShapeDtypeStruct((8, width), jnp.bfloat16)
        out_specs = whole((8, width))
        scratch = [pltpu.VMEM((8, width), jnp.float32)]
    else:
        out_shape = jax.ShapeDtypeStruct((rows, width), jnp.float32)
        out_specs = row_block
    hidden = 256 * count
    return pl.pallas_call(
        functools.partial(ffn_kernel, count, first, last),
        grid_spec=pltpu.PrefetchScalarGridSpec(
            num_scalar_prefetch=1,
            grid=(steps,),
            in_specs=in_specs,
            out_specs=out_specs,
            scratch_shapes=scratch,
        ),
        out_shape=out_shape,
        compiler_params=pltpu.CompilerParams(
            dimension_semantics=("arbitrary",), vmem_limit_bytes=56 * 2**20
        ),
        cost_estimate=pl.CostEstimate(
            flops=3 * rows * hidden * width, bytes_accessed=10 * 2**20, transcendentals=0
        ),
    )(meta, *operands)


def tail_kernel(place, *refs):
    pieces, refs = refs[:8], refs[8:]
    proj_ref, own_ref, slot_ref, gid_ref = refs[:4]
    loss_ref, grad_graph_ref, grad_text_ref, grad_proj_ref = refs[4:]
    flat, row_first = place[0], place[1]
    pooled = jnp.concatenate([p[...] for p in pieces], axis=0)
    texts = pooled.shape[0]
    graphs = gid_ref.shape[0]
    devices = texts // 8
    text_emb = jnp.dot(pooled, proj_ref[...], preferred_element_type=jnp.float32)
    text_norm = jnp.sqrt(jnp.sum(text_emb * text_emb, axis=-1, keepdims=True) + epsilon)
    text_unit = text_emb / text_norm
    text_send = text_unit.astype(jnp.bfloat16)
    line = lax.broadcasted_iota(jnp.int32, (2 * devices, texts), 0)
    wanted = jnp.where(line < devices, 8 * line + 6, 8 * (line - devices) + 7)
    carried = wanted == lax.broadcasted_iota(jnp.int32, (2 * devices, texts), 1)
    carriers = jnp.dot(
        carried.astype(jnp.bfloat16), pooled, preferred_element_type=jnp.float32
    ).astype(jnp.bfloat16)
    graph_send = jnp.concatenate(
        [carriers[0:devices, 256 * k : 256 * k + 256] for k in range(4)]
        + [carriers[devices:, 256 * k : 256 * k + 256] for k in range(2)],
        axis=0,
    )
    slot = slot_ref[...]
    valid = slot >= 0

    def scores(rows_send):
        logits = (
            lax.dot_general(rows_send, text_send, nt, preferred_element_type=jnp.float32)
            / sharpness_divisor
        )
        expo = jnp.where(valid, jnp.exp(logits), 0.0)
        return logits, expo, jnp.sum(expo, axis=1, keepdims=True)

    logits, expo, row_total = scores(graph_send)
    col_total = jnp.where(valid, jnp.sum(expo, axis=0, keepdims=True), 1.0)
    col_scale = 0.5 / col_total
    matched = gid_ref[...] == slot
    diagonal = jnp.sum(jnp.where(matched, logits, 0.0), axis=1, keepdims=True)
    row_terms = jnp.sum(jnp.log(row_total) - 2.0 * diagonal, axis=0, keepdims=True)
    col_terms = jnp.sum(jnp.log(col_total), axis=1, keepdims=True)
    loss_ref[...] = (row_terms + col_terms) / (2.0 * graphs)

    def weigh(expo, row_total, matched):
        weights = expo * (0.5 / row_total) + expo * col_scale
        return (weights - jnp.where(matched, 1.0, 0.0)).astype(jnp.bfloat16)

    weights = weigh(expo, row_total, matched)
    text_grad = (
        lax.dot_general(weights, graph_send, tn, preferred_element_type=jnp.float32)
        / sharpness_divisor
    )
    along = jnp.sum(text_unit * text_grad, axis=-1, keepdims=True)
    grad_text = (text_grad - text_unit * along) / text_norm
    grad_text_ref[...] = grad_text[0:8]

    own = own_ref[...]
    own_norm = jnp.sqrt(jnp.sum(own * own, axis=-1, keepdims=True) + epsilon)
    own_unit = own / own_norm
    _, own_expo, own_total = scores(own_unit.astype(jnp.bfloat16))
    own_rows = own.shape[0]
    own_matched = row_first + lax.broadcasted_iota(jnp.int32, (own_rows, texts), 0) == slot
    own_weights = weigh(own_expo, own_total, own_matched)
    graph_grad = (
        jnp.dot(own_weights, text_send, preferred_element_type=jnp.float32) / sharpness_divisor
    )
    own_along = jnp.sum(own_unit * graph_grad, axis=-1, keepdims=True)
    grad_graph_ref[...] = (graph_grad - own_unit * own_along) / own_norm

    width = pooled.shape[1]
    feature = lax.broadcasted_iota(jnp.int32, (width, 128), 0)
    wanted = flat * 8 + lax.broadcasted_iota(jnp.int32, (width, 128), 1)
    pick = (feature == wanted).astype(jnp.bfloat16)
    picked = jnp.dot(pooled, pick, preferred_element_type=jnp.float32)
    grad_proj = lax.dot_general(
        picked,
        grad_text,
        tn,
        precision=lax.Precision.HIGHEST,
        preferred_element_type=jnp.float32,
    )
    grad_proj_ref[...] = grad_proj[0:8]


def tail(place, pieces, proj_weight, graph_emb, slot, gid):
    shapes = [(1, 1), graph_emb.shape, (8, 256), (8, 256)]
    return pl.pallas_call(
        tail_kernel,
        in_specs=[pl.BlockSpec(memory_space=pltpu.SMEM)]
        + [pl.BlockSpec(memory_space=pltpu.VMEM)] * 12,
        out_specs=[pl.BlockSpec(memory_space=pltpu.VMEM)] * 4,
        out_shape=[jax.ShapeDtypeStruct(s, jnp.float32) for s in shapes],
        compiler_params=pltpu.CompilerParams(vmem_limit_bytes=48 * 2**20),
    )(place, *pieces, proj_weight, graph_emb, slot, gid)


def gather_weights(up_weight, up_bias, down_weight):
    width = up_weight.shape[1]
    bias = [jnp.tile(b.reshape(1, 16), (16, width // 16)) for b in (up_bias[:16], up_bias[16:])]
    own = jnp.concatenate([up_weight, down_weight, *bias], axis=0)
    halves = arrange(split_kernel, from_line(own, "dz"), 144)
    pieces = []
    for half, inner in zip(halves, ("dx", "dy")):
        ring = [half]
        for _ in range(3):
            ring.append(send(ring[-1], by_core=True, **{inner: 1}))
        pieces += ring
    pair = arrange(join_kernel, pieces, 528)
    pairs_in_order = [pair]
    for _ in range(3):
        pair = [
            send(block, by_core=True, **{outer: 1}) for block, outer in zip(pair, ("dy", "dx"))
        ]
        pairs_in_order.append(pair)
    return pairs_in_order


def shards(
    text_hidden, lengths, up_weight, up_bias, down_weight, ln_gain, proj_weight, graph_emb, perm
):
    row_index = lax.axis_index("row")
    col_index = lax.axis_index("col")
    z, y = row_index // 8, row_index % 4
    x = (col_index // 2) * 2 + (row_index // 4) % 2
    core = col_index % 2
    flat = row_index * 4 + col_index

    padded = (lengths + 15) // 16 * 16
    starts = jnp.cumsum(padded) - padded
    total = jnp.sum(padded)
    row_blocks = (total + block_rows - 1) // block_rows
    meta = jnp.concatenate(
        [starts, lengths, jnp.stack([total, row_blocks]), jnp.zeros((2,), jnp.int32)]
    ).astype(jnp.int32)

    packed = pack_tokens(meta, text_hidden)
    graph_norm = jnp.sqrt(jnp.sum(graph_emb * graph_emb, axis=-1, keepdims=True) + epsilon)
    graph_send = (graph_emb / graph_norm).astype(jnp.bfloat16)
    share = lax.dynamic_slice(graph_send, (col_index * 6, 0), (6, 256))
    share = jnp.pad(share, ((0, 2), (0, 0))).reshape(2, 1024)
    graph_rows = jnp.pad(share, ((6, 0), (0, 0)))

    mine = gather_weights(up_weight, up_bias, down_weight)
    other = [[send(block, dc=1) for block in pair] for pair in mine]
    step = functools.partial(ffn_step, meta, packed)
    acc = step(mine[0])
    acc = step(other[0] + mine[1], acc)
    acc = step(other[1] + mine[2], acc)
    acc = step(other[2], acc)
    acc = step(mine[3], acc)
    pooled = step(other[3], acc, ln_gain.reshape(1, -1), graph_rows)
    for axis in ("dz", "dy"):
        pooled = jnp.concatenate(from_line(pooled, axis), axis=0)
    line = from_line(pooled, "dx")
    pieces = line + [send(value, dc=1) for value in line]

    rel = jnp.array([0, -1, 1, 2], jnp.int32)
    ids = flat_index(
        ((x + rel) % 4)[None, :, None, None],
        ((y + rel) % 4)[None, None, :, None],
        ((z + rel) % 4)[None, None, None, :],
        (core ^ jnp.arange(2, dtype=jnp.int32))[:, None, None, None],
    ).reshape(-1, 1)
    lane = jnp.arange(8, dtype=jnp.int32)[None, :]
    tower = jnp.where(lane < 6, ids * 6 + lane, -1).reshape(-1)
    pairs_all = perm.shape[0]
    hit = tower[None, :] == jnp.arange(pairs_all, dtype=jnp.int32)[:, None]
    slot = jnp.sum(jnp.where(hit, perm[:, None] + 1, 0), axis=0, keepdims=True) - 1
    place = jnp.stack([flat, row_index * graph_emb.shape[0]]).astype(jnp.int32)
    gid = (ids.reshape(1, -1) * 6 + jnp.arange(6, dtype=jnp.int32)[:, None]).reshape(-1, 1)
    loss, grad_graph, grad_text, grad_proj = tail(
        place, pieces, proj_weight, graph_emb, slot.astype(jnp.int32), gid
    )
    return (loss[0, 0], grad_graph, grad_text[:6], grad_proj)


def solution(mesh):
    return jax.shard_map(
        shards,
        mesh=mesh,
        in_specs=(
            P(("row", "col"), None, None),
            P(("row", "col")),
            P(("row", "col"), None),
            P(("row", "col")),
            P(("row", "col"), None),
            P(),
            P(),
            P("row", None),
            P(),
        ),
        out_specs=(P(), P("row", None), P(("row", "col"), None), P(("row", "col"), None)),
        check_vma=False,
    )
```

```python
import functools

import jax
import jax.numpy as jnp
from jax import lax
from jax.experimental import pallas as pl
from jax.experimental.pallas import tpu as pltpu
from jax.sharding import PartitionSpec as P

sharpness_divisor = 0.02
epsilon = 1e-06
axes = ("row", "col")
block_rows = 256
erf_terms = (
    -5.7109417639367166e-08,
    2.812487991832313e-06,
    -4.7398178139701486e-05,
    -5.735534068662673e-05,
    0.03636491671204567,
    0.7978729605674744,
)
nt = (((1,), (1,)), ((), ()))
tn = (((0,), (0,)), ((), ()))


def flat_index(x, y, z, core):
    return (z * 8 + (x % 2) * 4 + y) * 4 + (x // 2) * 2 + core


def pairs(dx=0, dy=0, dz=0, dc=0, by_core=False):
    found = []
    for x in range(4):
        for y in range(4):
            for z in range(4):
                for core in range(2):
                    sign = -1 if by_core and core else 1
                    target = flat_index(
                        (x + sign * dx) % 4, (y + sign * dy) % 4, (z + sign * dz) % 4, core ^ dc
                    )
                    found.append((flat_index(x, y, z, core), target))
    return found


def send(value, **hop):
    return lax.ppermute(value, axes, pairs(**hop))


def from_line(value, axis):
    return [value] + [send(value, **{axis: hop}) for hop in (1, 3, 2)]


def gelu_exact(x):
    square = jnp.minimum(x * x, 25.0)
    series = jnp.full_like(square, erf_terms[0])
    for term in erf_terms[1:]:
        series = series * square + term
    half = 0.5 * x
    return half + half * jnp.tanh(x * series)


def pack_kernel(meta, source, packed, sem):
    for s in range(6):
        start = pl.multiple_of(meta[s], 16)
        copy = pltpu.make_async_copy(source.at[s], packed.at[pl.ds(start, 256)], sem)
        copy.start()
        copy.wait()


def pack_tokens(meta, text_hidden):
    seqs, seq_len, width = text_hidden.shape
    return pl.pallas_call(
        pack_kernel,
        grid_spec=pltpu.PrefetchScalarGridSpec(
            num_scalar_prefetch=1,
            grid=(),
            in_specs=[pl.BlockSpec(memory_space=pl.ANY)],
            out_specs=pl.BlockSpec(memory_space=pltpu.VMEM),
            scratch_shapes=[pltpu.SemaphoreType.DMA],
        ),
        out_shape=jax.ShapeDtypeStruct((seqs * seq_len, width), jnp.bfloat16),
        compiler_params=pltpu.CompilerParams(vmem_limit_bytes=16 * 2**20),
    )(meta, text_hidden)


def merge_bias(tiles, run):
    lane = lax.broadcasted_iota(jnp.int32, (1, tiles[0].shape[1]), 1) // run % 4
    row = tiles[0].astype(jnp.float32)[0:1]
    for k in range(1, 4):
        row = jnp.where(lane == k, tiles[k].astype(jnp.float32)[0:1], row)
    return jnp.broadcast_to(row, tiles[0].shape).astype(jnp.bfloat16)


def split_kernel(*refs):
    parts = refs[:4]
    for k, out in enumerate(refs[4:]):
        for s, part in enumerate(parts):
            out[16 * s : 16 * s + 16, :] = part[16 * k : 16 * k + 16, :]
            out[64 + 16 * s : 80 + 16 * s, :] = part[32 + 16 * k : 48 + 16 * k, :]
        out[128:144, :] = merge_bias([p[64 + 16 * k : 80 + 16 * k, :] for p in parts], 16)


def join_kernel(*refs):
    for k, out in enumerate(refs[8:]):
        parts = refs[4 * k : 4 * k + 4]
        for s, part in enumerate(parts):
            out[64 * s : 64 * s + 64, :] = part[0:64, :]
            out[256 + 64 * s : 320 + 64 * s, :] = part[64:128, :]
        out[512:528, :] = merge_bias([p[128:144, :] for p in parts], 64)


def arrange(body, parts, rows):
    shape = jax.ShapeDtypeStruct((rows, parts[0].shape[1]), jnp.bfloat16)
    return pl.pallas_call(
        body,
        in_specs=[pl.BlockSpec(memory_space=pltpu.VMEM)] * len(parts),
        out_specs=[pl.BlockSpec(memory_space=pltpu.VMEM)] * 2,
        out_shape=[shape, shape],
        compiler_params=pltpu.CompilerParams(vmem_limit_bytes=16 * 2**20),
    )(*parts)


def ffn_tiles(x, weights):
    up = jnp.concatenate([w[0:256, :] for w in weights], axis=0)
    down = jnp.concatenate([w[256:512, :] for w in weights], axis=0)
    bias = jnp.concatenate(
        [w[512:528, 0:256].astype(jnp.float32)[0:1] for w in weights], axis=1
    )
    preact = lax.dot_general(x, up, nt, preferred_element_type=jnp.float32) + bias
    active = gelu_exact(preact).astype(jnp.bfloat16)
    return jnp.dot(active, down, preferred_element_type=jnp.float32)


def ffn_kernel(count, first, last, meta, x_ref, *refs):
    weights, refs = refs[:count], refs[count:]
    if not first:
        acc_in, refs = refs[0], refs[1:]
    if last:
        gain_ref, graph_ref, pooled_ref, sums = refs
        sums[...] = jnp.zeros_like(sums)
    else:
        (out_ref,) = refs

    def rows_step(base, height):
        at = pl.ds(pl.multiple_of(base, block_rows), height)
        x = x_ref[at, :]
        total = ffn_tiles(x, weights)
        if not first:
            total = acc_in[at, :] + total
        if not last:
            out_ref[at, :] = total
            return
        summed = x.astype(jnp.float32) + total
        centre = summed - jnp.mean(summed, axis=-1, keepdims=True)
        spread = jnp.mean(centre * centre, axis=-1, keepdims=True)
        normed = centre * lax.rsqrt(spread + epsilon) * gain_ref[...]
        row = base + lax.broadcasted_iota(jnp.int32, (height, 1), 0)
        normed = jnp.where(row < meta[12], normed, 0.0)
        column = base + lax.broadcasted_iota(jnp.int32, (8, height), 1)
        seq = lax.broadcasted_iota(jnp.int32, (8, height), 0)
        member = jnp.zeros((8, height), jnp.float32)
        for s in range(6):
            inside = (column >= meta[s]) & (column < meta[s] + meta[6 + s]) & (seq == s)
            member = jnp.where(inside, 1.0, member)
        sums[...] += jnp.dot(
            member, normed, precision=lax.Precision.HIGHEST, preferred_element_type=jnp.float32
        )

    blocks = meta[13]
    double = 2 * block_rows

    @pl.loop(0, blocks // 2)
    def _(i):
        rows_step(i * double, double)

    @pl.when(blocks % 2 == 1)
    def _():
        rows_step((blocks - 1) * block_rows, block_rows)

    if last:
        seq = lax.broadcasted_iota(jnp.int32, (8, 1), 0)
        tokens = jnp.ones((8, 1), jnp.float32)
        for s in range(6):
            tokens = jnp.where(seq == s, meta[6 + s].astype(jnp.float32), tokens)
        means = (sums[...] / tokens).astype(jnp.bfloat16)
        pooled_ref[...] = jnp.where(seq < 6, means, graph_ref[...])


def ffn_step(meta, packed, weights, acc=None, gain=None, graph_rows=None):
    rows, width = packed.shape
    count, first, last = len(weights), acc is None, gain is not None
    operands = [packed, *weights]
    aliases = {}
    if not first:
        if not last:
            aliases = {1 + len(operands): 0}
        operands.append(acc)
    scratch = []
    if last:
        operands += [gain, graph_rows]
        out_shape = jax.ShapeDtypeStruct((8, width), jnp.bfloat16)
        scratch = [pltpu.VMEM((8, width), jnp.float32)]
    else:
        out_shape = jax.ShapeDtypeStruct((rows, width), jnp.float32)
    return pl.pallas_call(
        functools.partial(ffn_kernel, count, first, last),
        in_specs=[pl.BlockSpec(memory_space=pltpu.SMEM)]
        + [pl.BlockSpec(memory_space=pltpu.VMEM)] * len(operands),
        out_specs=pl.BlockSpec(memory_space=pltpu.VMEM),
        scratch_shapes=scratch,
        out_shape=out_shape,
        input_output_aliases=aliases,
        compiler_params=pltpu.CompilerParams(vmem_limit_bytes=24 * 2**20),
        cost_estimate=pl.CostEstimate(
            flops=4 * rows * 256 * count * width, bytes_accessed=2**20, transcendentals=0
        ),
    )(meta, *operands)


def tie_kernel(*refs):
    del refs


def after(values, done):
    return pl.pallas_call(
        tie_kernel,
        in_specs=[pl.BlockSpec(memory_space=pl.ANY)] * (len(values) + 1),
        out_specs=[pl.BlockSpec(memory_space=pl.ANY)] * len(values),
        out_shape=[jax.ShapeDtypeStruct(v.shape, v.dtype) for v in values],
        input_output_aliases={k: k for k in range(len(values))},
    )(*values, done)


def tail_kernel(place, *refs):
    pieces, refs = refs[:8], refs[8:]
    proj_ref, own_ref, slot_ref, gid_ref = refs[:4]
    loss_ref, grad_graph_ref, grad_text_ref, grad_proj_ref = refs[4:]
    flat, row_first = place[0], place[1]
    pooled = jnp.concatenate([p[...] for p in pieces], axis=0)
    texts = pooled.shape[0]
    graphs = gid_ref.shape[0]
    devices = texts // 8
    text_emb = jnp.dot(pooled, proj_ref[...], preferred_element_type=jnp.float32)
    text_norm = jnp.sqrt(jnp.sum(text_emb * text_emb, axis=-1, keepdims=True) + epsilon)
    text_unit = text_emb / text_norm
    text_send = text_unit.astype(jnp.bfloat16)
    line = lax.broadcasted_iota(jnp.int32, (2 * devices, texts), 0)
    wanted = jnp.where(line < devices, 8 * line + 6, 8 * (line - devices) + 7)
    carried = wanted == lax.broadcasted_iota(jnp.int32, (2 * devices, texts), 1)
    carriers = jnp.dot(
        carried.astype(jnp.bfloat16), pooled, preferred_element_type=jnp.float32
    ).astype(jnp.bfloat16)
    graph_send = jnp.concatenate(
        [carriers[0:devices, 256 * k : 256 * k + 256] for k in range(4)]
        + [carriers[devices:, 256 * k : 256 * k + 256] for k in range(2)],
        axis=0,
    )
    slot = slot_ref[...]
    valid = slot >= 0

    def scores(rows_send):
        logits = (
            lax.dot_general(rows_send, text_send, nt, preferred_element_type=jnp.float32)
            / sharpness_divisor
        )
        expo = jnp.where(valid, jnp.exp(logits), 0.0)
        return logits, expo, jnp.sum(expo, axis=1, keepdims=True)

    logits, expo, row_total = scores(graph_send)
    col_total = jnp.where(valid, jnp.sum(expo, axis=0, keepdims=True), 1.0)
    col_scale = 0.5 / col_total
    matched = gid_ref[...] == slot
    diagonal = jnp.sum(jnp.where(matched, logits, 0.0), axis=1, keepdims=True)
    row_terms = jnp.sum(jnp.log(row_total) - 2.0 * diagonal, axis=0, keepdims=True)
    col_terms = jnp.sum(jnp.log(col_total), axis=1, keepdims=True)
    loss_ref[...] = (row_terms + col_terms) / (2.0 * graphs)

    def weigh(expo, row_total, matched):
        weights = expo * (0.5 / row_total) + expo * col_scale
        return (weights - jnp.where(matched, 1.0, 0.0)).astype(jnp.bfloat16)

    weights = weigh(expo, row_total, matched)
    text_grad = (
        lax.dot_general(weights, graph_send, tn, preferred_element_type=jnp.float32)
        / sharpness_divisor
    )
    along = jnp.sum(text_unit * text_grad, axis=-1, keepdims=True)
    grad_text = (text_grad - text_unit * along) / text_norm
    grad_text_ref[...] = grad_text[0:8]

    own = own_ref[...]
    own_norm = jnp.sqrt(jnp.sum(own * own, axis=-1, keepdims=True) + epsilon)
    own_unit = own / own_norm
    _, own_expo, own_total = scores(own_unit.astype(jnp.bfloat16))
    own_rows = own.shape[0]
    own_matched = row_first + lax.broadcasted_iota(jnp.int32, (own_rows, texts), 0) == slot
    own_weights = weigh(own_expo, own_total, own_matched)
    graph_grad = (
        jnp.dot(own_weights, text_send, preferred_element_type=jnp.float32) / sharpness_divisor
    )
    own_along = jnp.sum(own_unit * graph_grad, axis=-1, keepdims=True)
    grad_graph_ref[...] = (graph_grad - own_unit * own_along) / own_norm

    width = pooled.shape[1]
    feature = lax.broadcasted_iota(jnp.int32, (width, 128), 0)
    wanted = flat * 8 + lax.broadcasted_iota(jnp.int32, (width, 128), 1)
    pick = (feature == wanted).astype(jnp.bfloat16)
    picked = jnp.dot(pooled, pick, preferred_element_type=jnp.float32)
    grad_proj = lax.dot_general(
        picked,
        grad_text,
        tn,
        precision=lax.Precision.HIGHEST,
        preferred_element_type=jnp.float32,
    )
    grad_proj_ref[...] = grad_proj[0:8]


def tail(place, pieces, proj_weight, graph_emb, slot, gid):
    shapes = [(1, 1), graph_emb.shape, (8, 256), (8, 256)]
    return pl.pallas_call(
        tail_kernel,
        in_specs=[pl.BlockSpec(memory_space=pltpu.SMEM)]
        + [pl.BlockSpec(memory_space=pltpu.VMEM)] * 12,
        out_specs=[pl.BlockSpec(memory_space=pltpu.VMEM)] * 4,
        out_shape=[jax.ShapeDtypeStruct(s, jnp.float32) for s in shapes],
        compiler_params=pltpu.CompilerParams(vmem_limit_bytes=48 * 2**20),
    )(place, *pieces, proj_weight, graph_emb, slot, gid)


def gather_weights(up_weight, up_bias, down_weight):
    width = up_weight.shape[1]
    bias = [jnp.tile(b.reshape(1, 16), (16, width // 16)) for b in (up_bias[:16], up_bias[16:])]
    own = jnp.concatenate([up_weight, down_weight, *bias], axis=0)
    halves = arrange(split_kernel, from_line(own, "dz"), 144)
    pieces = []
    for half, inner in zip(halves, ("dx", "dy")):
        ring = [half]
        for _ in range(3):
            ring.append(send(ring[-1], by_core=True, **{inner: 1}))
        pieces += ring
    return arrange(join_kernel, pieces, 528)


def shards(
    text_hidden, lengths, up_weight, up_bias, down_weight, ln_gain, proj_weight, graph_emb, perm
):
    row_index = lax.axis_index("row")
    col_index = lax.axis_index("col")
    z, y = row_index // 8, row_index % 4
    x = (col_index // 2) * 2 + (row_index // 4) % 2
    core = col_index % 2
    flat = row_index * 4 + col_index

    padded = (lengths + 15) // 16 * 16
    starts = jnp.cumsum(padded) - padded
    total = jnp.sum(padded)
    row_blocks = (total + block_rows - 1) // block_rows
    meta = jnp.concatenate(
        [starts, lengths, jnp.stack([total, row_blocks]), jnp.zeros((2,), jnp.int32)]
    ).astype(jnp.int32)

    packed = pack_tokens(meta, text_hidden)
    graph_norm = jnp.sqrt(jnp.sum(graph_emb * graph_emb, axis=-1, keepdims=True) + epsilon)
    graph_send = (graph_emb / graph_norm).astype(jnp.bfloat16)
    share = lax.dynamic_slice(graph_send, (col_index * 6, 0), (6, 256))
    share = jnp.pad(share, ((0, 2), (0, 0))).reshape(2, 1024)
    graph_rows = jnp.pad(share, ((6, 0), (0, 0)))

    mine = gather_weights(up_weight, up_bias, down_weight)
    step = functools.partial(ffn_step, meta, packed)
    acc = None
    for turn in range(4):
        other = [send(block, dc=1) for block in mine]
        if turn < 3:
            coming = [
                send(block, by_core=True, **{outer: 1}) for block, outer in zip(mine, ("dy", "dx"))
            ]
        acc = step(mine, acc)
        if turn < 3:
            acc = step(other, acc)
            mine = after(coming, acc)
    pooled = step(other, acc, ln_gain.reshape(1, -1), graph_rows)
    for axis in ("dz", "dy"):
        pooled = jnp.concatenate(from_line(pooled, axis), axis=0)
    line = from_line(pooled, "dx")
    pieces = line + [send(value, dc=1) for value in line]

    rel = jnp.array([0, -1, 1, 2], jnp.int32)
    ids = flat_index(
        ((x + rel) % 4)[None, :, None, None],
        ((y + rel) % 4)[None, None, :, None],
        ((z + rel) % 4)[None, None, None, :],
        (core ^ jnp.arange(2, dtype=jnp.int32))[:, None, None, None],
    ).reshape(-1, 1)
    lane = jnp.arange(8, dtype=jnp.int32)[None, :]
    tower = jnp.where(lane < 6, ids * 6 + lane, -1).reshape(-1)
    pairs_all = perm.shape[0]
    hit = tower[None, :] == jnp.arange(pairs_all, dtype=jnp.int32)[:, None]
    slot = jnp.sum(jnp.where(hit, perm[:, None] + 1, 0), axis=0, keepdims=True) - 1
    place = jnp.stack([flat, row_index * graph_emb.shape[0]]).astype(jnp.int32)
    gid = (ids.reshape(1, -1) * 6 + jnp.arange(6, dtype=jnp.int32)[:, None]).reshape(-1, 1)
    loss, grad_graph, grad_text, grad_proj = tail(
        place, pieces, proj_weight, graph_emb, slot.astype(jnp.int32), gid
    )
    return (loss[0, 0], grad_graph, grad_text[:6], grad_proj)


def solution(mesh):
    return jax.shard_map(
        shards,
        mesh=mesh,
        in_specs=(
            P(("row", "col"), None, None),
            P(("row", "col")),
            P(("row", "col"), None),
            P(("row", "col")),
            P(("row", "col"), None),
            P(),
            P(),
            P("row", None),
            P(),
        ),
        out_specs=(P(), P("row", None), P(("row", "col"), None), P(("row", "col"), None)),
        check_vma=False,
    )
```

```python
import functools

import jax
import jax.numpy as jnp
from jax import lax
from jax.experimental import pallas as pl
from jax.experimental.pallas import tpu as pltpu
from jax.sharding import PartitionSpec as P

sharpness_divisor = 0.02
epsilon = 1e-06
axes = ("row", "col")
block_rows = 256
erf_terms = (
    -5.7109417639367166e-08,
    2.812487991832313e-06,
    -4.7398178139701486e-05,
    -5.735534068662673e-05,
    0.03636491671204567,
    0.7978729605674744,
)
nt = (((1,), (1,)), ((), ()))
tn = (((0,), (0,)), ((), ()))


def flat_index(x, y, z, core):
    return (z * 8 + (x % 2) * 4 + y) * 4 + (x // 2) * 2 + core


def pairs(dx=0, dy=0, dz=0, dc=0, by_core=False):
    found = []
    for x in range(4):
        for y in range(4):
            for z in range(4):
                for core in range(2):
                    sign = -1 if by_core and core else 1
                    target = flat_index(
                        (x + sign * dx) % 4, (y + sign * dy) % 4, (z + sign * dz) % 4, core ^ dc
                    )
                    found.append((flat_index(x, y, z, core), target))
    return found


def send(value, **hop):
    return lax.ppermute(value, axes, pairs(**hop))


def from_line(value, axis):
    return [value] + [send(value, **{axis: hop}) for hop in (1, 3, 2)]


def gelu_exact(x):
    square = jnp.minimum(x * x, 25.0)
    series = jnp.full_like(square, erf_terms[0])
    for term in erf_terms[1:]:
        series = series * square + term
    half = 0.5 * x
    return half + half * jnp.tanh(x * series)


def spot(x, y, z, core, order):
    def away(here, step):
        moved = jnp.where(step == 1, 3, jnp.where(step == 2, 1, jnp.where(step == 3, 2, 0)))
        return (here + moved) & 3

    x, y = away(x, (order >> 4) & 3), away(y, (order >> 2) & 3)
    z, core = away(z, order & 3), core ^ ((order >> 6) & 1)
    return (z * 8 + (x & 1) * 4 + y) * 4 + (x >> 1) * 2 + core


def prepare_kernel(
    lengths, tokens_ref, perm_ref, graph_ref, meta, place, packed, slot_ref, gid_ref, rows_ref, sem
):
    row, col = lax.axis_index("row"), lax.axis_index("col")
    z, y, core = row >> 3, row & 3, col & 1
    x = (col >> 1) * 2 + ((row >> 2) & 1)
    place[0] = row * 4 + col
    place[1] = row * graph_ref.shape[0]
    start = jnp.int32(0)
    for s in range(6):
        meta[s] = start
        meta[6 + s] = lengths[s]
        begin = pl.multiple_of(start, 16)
        copy = pltpu.make_async_copy(tokens_ref.at[s], packed.at[pl.ds(begin, 256)], sem)
        copy.start()
        copy.wait()
        start = start + ((lengths[s] + 15) >> 4 << 4)
    meta[12] = start
    meta[13] = (start + block_rows - 1) // block_rows
    meta[14] = 0
    meta[15] = 0

    count, texts = perm_ref.shape[1], slot_ref.shape[1]
    text = lax.broadcasted_iota(jnp.int32, (1, texts), 1)
    member = text & 7
    device = spot(x, y, z, core, text >> 3)
    tower = jnp.where(member < 6, device * 6 + member, -1)
    hit = lax.broadcasted_iota(jnp.int32, (count, texts), 0) == tower
    perm = perm_ref[...]
    high, low = (perm >> 5).astype(jnp.float32), (perm & 31).astype(jnp.float32)
    line = lax.broadcasted_iota(jnp.int32, (16, count), 0)
    digits = jnp.where(line == 0, high, jnp.where(line == 1, low, 0.0)).astype(jnp.bfloat16)
    found = jnp.dot(digits, hit.astype(jnp.bfloat16), preferred_element_type=jnp.float32)
    slot = (found[0:1] * 32.0 + found[1:2]).astype(jnp.int32)
    slot_ref[...] = jnp.where(tower >= 0, slot, -1)
    graph = lax.broadcasted_iota(jnp.int32, gid_ref.shape, 0)
    gid_ref[...] = spot(x, y, z, core, graph & 127) * 6 + (graph >> 7)

    own = graph_ref[...]
    norm = jnp.sqrt(jnp.sum(own * own, axis=-1, keepdims=True) + epsilon)
    unit = (own / norm).astype(jnp.bfloat16)
    take = lax.broadcasted_iota(jnp.int32, (16, own.shape[0]), 0) + col * 6
    take = take == lax.broadcasted_iota(jnp.int32, (16, own.shape[0]), 1)
    share = jnp.dot(take.astype(jnp.bfloat16), unit, preferred_element_type=jnp.float32)
    first = jnp.concatenate([share[k : k + 1] for k in range(4)], axis=1)
    second = jnp.concatenate([share[k : k + 1] for k in (4, 5)] * 2, axis=1)
    at = lax.broadcasted_iota(jnp.int32, rows_ref.shape, 0)
    rows_ref[...] = jnp.where(at == 6, first, jnp.where(at == 7, second, 0.0)).astype(jnp.bfloat16)


def prepare(text_hidden, lengths, perm, graph_emb):
    seqs, seq_len, width = text_hidden.shape
    count = perm.shape[0]
    smem, vmem = pl.BlockSpec(memory_space=pltpu.SMEM), pl.BlockSpec(memory_space=pltpu.VMEM)
    return pl.pallas_call(
        prepare_kernel,
        in_specs=[smem, pl.BlockSpec(memory_space=pl.ANY), vmem, vmem],
        out_specs=[smem, smem, vmem, vmem, vmem, vmem],
        out_shape=[
            jax.ShapeDtypeStruct((16,), jnp.int32),
            jax.ShapeDtypeStruct((2,), jnp.int32),
            jax.ShapeDtypeStruct((seqs * seq_len, width), jnp.bfloat16),
            jax.ShapeDtypeStruct((1, count // 6 * 8), jnp.int32),
            jax.ShapeDtypeStruct((count, 1), jnp.int32),
            jax.ShapeDtypeStruct((8, width), jnp.bfloat16),
        ],
        scratch_shapes=[pltpu.SemaphoreType.DMA],
        compiler_params=pltpu.CompilerParams(vmem_limit_bytes=12 * 2**20),
    )(lengths, text_hidden, perm.reshape(1, count), graph_emb)


def merge_bias(tiles, run):
    lane = lax.broadcasted_iota(jnp.int32, (1, tiles[0].shape[1]), 1) // run % 4
    row = tiles[0].astype(jnp.float32)[0:1]
    for k in range(1, 4):
        row = jnp.where(lane == k, tiles[k].astype(jnp.float32)[0:1], row)
    return jnp.broadcast_to(row, tiles[0].shape).astype(jnp.bfloat16)


def split_kernel(*refs):
    parts = refs[:4]
    for k, out in enumerate(refs[-2:]):
        for s, part in enumerate(parts):
            out[16 * s : 16 * s + 16, :] = part[16 * k : 16 * k + 16, :]
            out[64 + 16 * s : 80 + 16 * s, :] = part[32 + 16 * k : 48 + 16 * k, :]
        out[128:144, :] = merge_bias([p[64 + 16 * k : 80 + 16 * k, :] for p in parts], 16)


def join_kernel(*refs):
    for k, out in enumerate(refs[8:]):
        parts = refs[4 * k : 4 * k + 4]
        for s, part in enumerate(parts):
            out[64 * s : 64 * s + 64, :] = part[0:64, :]
            out[256 + 64 * s : 320 + 64 * s, :] = part[64:128, :]
        out[512:528, :] = merge_bias([p[128:144, :] for p in parts], 64)


def arrange(body, parts, rows, done=()):
    shape = jax.ShapeDtypeStruct((rows, parts[0].shape[1]), jnp.bfloat16)
    return pl.pallas_call(
        body,
        in_specs=[pl.BlockSpec(memory_space=pltpu.VMEM)] * len(parts)
        + [pl.BlockSpec(memory_space=pl.ANY)] * len(done),
        out_specs=[pl.BlockSpec(memory_space=pltpu.VMEM)] * 2,
        out_shape=[shape, shape],
        compiler_params=pltpu.CompilerParams(vmem_limit_bytes=4 * 2**20),
    )(*parts, *done)


def ffn_tiles(x, weights):
    up = jnp.concatenate([w[0:256, :] for w in weights], axis=0)
    down = jnp.concatenate([w[256:512, :] for w in weights], axis=0)
    bias = jnp.concatenate(
        [w[512:528, 0:256].astype(jnp.float32)[0:1] for w in weights], axis=1
    )
    preact = lax.dot_general(x, up, nt, preferred_element_type=jnp.float32) + bias
    active = gelu_exact(preact).astype(jnp.bfloat16)
    return jnp.dot(active, down, preferred_element_type=jnp.float32)


def ffn_kernel(count, first, last, meta, x_ref, *refs):
    weights, refs = refs[:count], refs[count:]
    if not first:
        acc_in, refs = refs[0], refs[1:]
    if last:
        gain_ref, graph_ref, pooled_ref, sums = refs
        sums[...] = jnp.zeros_like(sums)
    else:
        out_ref, token_ref = refs
        token_ref[...] = jnp.zeros_like(token_ref)

    def rows_step(base, height):
        at = pl.ds(pl.multiple_of(base, block_rows), height)
        x = x_ref[at, :]
        total = ffn_tiles(x, weights)
        if not first:
            total = acc_in[at, :] + total
        if not last:
            out_ref[at, :] = total
            return
        summed = x.astype(jnp.float32) + total
        centre = summed - jnp.mean(summed, axis=-1, keepdims=True)
        spread = jnp.mean(centre * centre, axis=-1, keepdims=True)
        normed = centre * lax.rsqrt(spread + epsilon) * gain_ref[...]
        row = base + lax.broadcasted_iota(jnp.int32, (height, 1), 0)
        groups = height // 16
        group = base + 16 * lax.broadcasted_iota(jnp.int32, (8, groups), 1)
        seq = lax.broadcasted_iota(jnp.int32, (8, groups), 0)
        valid = row < 0
        member = group < 0
        for s in range(6):
            start, stop = meta[s], meta[s] + meta[6 + s]
            valid |= (row >= start) & (row < stop)
            member |= (group >= start) & (group < stop) & (seq == s)
        normed = jnp.where(valid, normed, 0.0)
        partial = jnp.sum(normed.reshape(groups, 16, normed.shape[1]), axis=1)
        sums[...] += jnp.dot(
            member.astype(jnp.float32),
            partial,
            precision=lax.Precision.HIGHEST,
            preferred_element_type=jnp.float32,
        )

    blocks = meta[13]
    double = 2 * block_rows

    @pl.loop(0, blocks // 2)
    def _(i):
        rows_step(i * double, double)

    @pl.when(blocks % 2 == 1)
    def _():
        rows_step((blocks - 1) * block_rows, block_rows)

    if last:
        seq = lax.broadcasted_iota(jnp.int32, (8, 1), 0)
        tokens = jnp.ones((8, 1), jnp.float32)
        for s in range(6):
            tokens = jnp.where(seq == s, meta[6 + s].astype(jnp.float32), tokens)
        means = (sums[...] / tokens).astype(jnp.bfloat16)
        pooled_ref[...] = jnp.where(seq < 6, means, graph_ref[...])


def ffn_step(meta, packed, weights, acc=None, gain=None, graph_rows=None):
    rows, width = packed.shape
    count, first, last = len(weights), acc is None, gain is not None
    operands = [packed, *weights]
    aliases = {}
    if not first:
        if not last:
            aliases = {1 + len(operands): 0}
        operands.append(acc)
    scratch = []
    if last:
        operands += [gain, graph_rows]
        out_shape = jax.ShapeDtypeStruct((8, width), jnp.bfloat16)
        scratch = [pltpu.VMEM((8, width), jnp.float32)]
    else:
        out_shape = [jax.ShapeDtypeStruct((rows, width), jnp.float32)]
        out_shape.append(jax.ShapeDtypeStruct((8, 128), jnp.float32))
    vmem = pl.BlockSpec(memory_space=pltpu.VMEM)
    return pl.pallas_call(
        functools.partial(ffn_kernel, count, first, last),
        in_specs=[pl.BlockSpec(memory_space=pltpu.SMEM)]
        + [pl.BlockSpec(memory_space=pltpu.VMEM)] * len(operands),
        out_specs=vmem if last else [vmem, vmem],
        scratch_shapes=scratch,
        out_shape=out_shape,
        input_output_aliases=aliases,
        compiler_params=pltpu.CompilerParams(vmem_limit_bytes=8 * 2**20),
        cost_estimate=pl.CostEstimate(
            flops=4 * rows * 256 * count * width, bytes_accessed=2**20, transcendentals=0
        ),
    )(meta, *operands)


def tie_kernel(*refs):
    del refs


def after(values, done):
    return pl.pallas_call(
        tie_kernel,
        in_specs=[pl.BlockSpec(memory_space=pl.ANY)] * (len(values) + 1),
        out_specs=[pl.BlockSpec(memory_space=pl.ANY)] * len(values),
        out_shape=[jax.ShapeDtypeStruct(v.shape, v.dtype) for v in values],
        input_output_aliases={k: k for k in range(len(values))},
        compiler_params=pltpu.CompilerParams(vmem_limit_bytes=2**20),
    )(*values, done)


def tail_kernel(place, *refs):
    pieces, refs = refs[:8], refs[8:]
    proj_ref, own_ref, slot_ref, gid_ref = refs[:4]
    loss_ref, grad_graph_ref, grad_text_ref, grad_proj_ref = refs[4:]
    flat, row_first = place[0], place[1]
    pooled = jnp.concatenate([p[...] for p in pieces], axis=0)
    texts = pooled.shape[0]
    graphs = gid_ref.shape[0]
    devices = texts // 8
    text_emb = jnp.dot(pooled, proj_ref[...], preferred_element_type=jnp.float32)
    text_norm = jnp.sqrt(jnp.sum(text_emb * text_emb, axis=-1, keepdims=True) + epsilon)
    text_unit = text_emb / text_norm
    text_send = text_unit.astype(jnp.bfloat16)
    line = lax.broadcasted_iota(jnp.int32, (2 * devices, texts), 0)
    wanted = jnp.where(line < devices, 8 * line + 6, 8 * (line - devices) + 7)
    carried = wanted == lax.broadcasted_iota(jnp.int32, (2 * devices, texts), 1)
    carriers = jnp.dot(
        carried.astype(jnp.bfloat16), pooled, preferred_element_type=jnp.float32
    ).astype(jnp.bfloat16)
    graph_send = jnp.concatenate(
        [carriers[0:devices, 256 * k : 256 * k + 256] for k in range(4)]
        + [carriers[devices:, 256 * k : 256 * k + 256] for k in range(2)],
        axis=0,
    )
    slot = slot_ref[...]
    valid = slot >= 0

    def scores(rows_send):
        logits = (
            lax.dot_general(rows_send, text_send, nt, preferred_element_type=jnp.float32)
            / sharpness_divisor
        )
        expo = jnp.where(valid, jnp.exp(logits), 0.0)
        return logits, expo, jnp.sum(expo, axis=1, keepdims=True)

    logits, expo, row_total = scores(graph_send)
    col_total = jnp.where(valid, jnp.sum(expo, axis=0, keepdims=True), 1.0)
    col_scale = 0.5 / col_total
    matched = gid_ref[...] == slot
    diagonal = jnp.sum(jnp.where(matched, logits, 0.0), axis=1, keepdims=True)
    row_terms = jnp.sum(jnp.log(row_total) - 2.0 * diagonal, axis=0, keepdims=True)
    col_terms = jnp.sum(jnp.log(col_total), axis=1, keepdims=True)
    loss_ref[...] = (row_terms + col_terms) / (2.0 * graphs)

    def weigh(expo, row_total, matched):
        weights = expo * (0.5 / row_total) + expo * col_scale
        return (weights - jnp.where(matched, 1.0, 0.0)).astype(jnp.bfloat16)

    weights = weigh(expo, row_total, matched)
    text_grad = (
        lax.dot_general(weights, graph_send, tn, preferred_element_type=jnp.float32)
        / sharpness_divisor
    )
    along = jnp.sum(text_unit * text_grad, axis=-1, keepdims=True)
    grad_text = (text_grad - text_unit * along) / text_norm
    grad_text_ref[...] = grad_text[0:8]

    own = own_ref[...]
    own_norm = jnp.sqrt(jnp.sum(own * own, axis=-1, keepdims=True) + epsilon)
    own_unit = own / own_norm
    _, own_expo, own_total = scores(own_unit.astype(jnp.bfloat16))
    own_rows = own.shape[0]
    own_matched = row_first + lax.broadcasted_iota(jnp.int32, (own_rows, texts), 0) == slot
    own_weights = weigh(own_expo, own_total, own_matched)
    graph_grad = (
        jnp.dot(own_weights, text_send, preferred_element_type=jnp.float32) / sharpness_divisor
    )
    own_along = jnp.sum(own_unit * graph_grad, axis=-1, keepdims=True)
    grad_graph_ref[...] = (graph_grad - own_unit * own_along) / own_norm

    width = pooled.shape[1]
    feature = lax.broadcasted_iota(jnp.int32, (width, 128), 0)
    wanted = flat * 8 + lax.broadcasted_iota(jnp.int32, (width, 128), 1)
    pick = (feature == wanted).astype(jnp.bfloat16)
    picked = jnp.dot(pooled, pick, preferred_element_type=jnp.float32)
    grad_proj = lax.dot_general(
        picked,
        grad_text,
        tn,
        precision=lax.Precision.HIGHEST,
        preferred_element_type=jnp.float32,
    )
    grad_proj_ref[...] = grad_proj[0:8]


def tail(place, pieces, proj_weight, graph_emb, slot, gid):
    shapes = [(1, 1), graph_emb.shape, (8, 256), (8, 256)]
    return pl.pallas_call(
        tail_kernel,
        in_specs=[pl.BlockSpec(memory_space=pltpu.SMEM)]
        + [pl.BlockSpec(memory_space=pltpu.VMEM)] * 12,
        out_specs=[pl.BlockSpec(memory_space=pltpu.VMEM)] * 4,
        out_shape=[jax.ShapeDtypeStruct(s, jnp.float32) for s in shapes],
        compiler_params=pltpu.CompilerParams(vmem_limit_bytes=48 * 2**20),
    )(place, *pieces, proj_weight, graph_emb, slot, gid)


def gather_weights(up_weight, up_bias, down_weight, done):
    width = up_weight.shape[1]
    bias = [jnp.tile(b.reshape(1, 16), (16, width // 16)) for b in (up_bias[:16], up_bias[16:])]
    own = jnp.concatenate([up_weight, down_weight, *bias], axis=0)
    halves = arrange(split_kernel, from_line(own, "dz"), 144, (done,))
    pieces = []
    for half, inner in zip(halves, ("dx", "dy")):
        ring = [half]
        for _ in range(3):
            ring.append(send(ring[-1], by_core=True, **{inner: 1}))
        pieces += ring
    return arrange(join_kernel, pieces, 528)


def shards(
    text_hidden, lengths, up_weight, up_bias, down_weight, ln_gain, proj_weight, graph_emb, perm
):
    meta, place, packed, slot, gid, graph_rows = prepare(text_hidden, lengths, perm, graph_emb)
    mine = gather_weights(up_weight, up_bias, down_weight, graph_rows)
    step = functools.partial(ffn_step, meta, packed)
    acc = None
    for turn in range(4):
        other = [send(block, dc=1) for block in mine]
        if turn < 3:
            coming = [
                send(block, by_core=True, **{outer: 1}) for block, outer in zip(mine, ("dy", "dx"))
            ]
        acc, _ = step(mine, acc)
        if turn < 3:
            acc, token = step(other, acc)
            mine = after(coming, token)
    pooled = step(other, acc, ln_gain.reshape(1, -1), graph_rows)
    for axis in ("dz", "dy"):
        pooled = jnp.concatenate(from_line(pooled, axis), axis=0)
    line = from_line(pooled, "dx")
    pieces = line + [send(value, dc=1) for value in line]

    loss, grad_graph, grad_text, grad_proj = tail(
        place, pieces, proj_weight, graph_emb, slot, gid
    )
    return (loss[0, 0], grad_graph, grad_text[:6], grad_proj)


def solution(mesh):
    return jax.shard_map(
        shards,
        mesh=mesh,
        in_specs=(
            P(("row", "col"), None, None),
            P(("row", "col")),
            P(("row", "col"), None),
            P(("row", "col")),
            P(("row", "col"), None),
            P(),
            P(),
            P("row", None),
            P(),
        ),
        out_specs=(P(), P("row", None), P(("row", "col"), None), P(("row", "col"), None)),
        check_vma=False,
    )
```

```python
import functools

import jax
import jax.numpy as jnp
from jax import lax
from jax.experimental import pallas as pl
from jax.experimental.pallas import tpu as pltpu
from jax.sharding import PartitionSpec as P

sharpness = 1.0 / 0.02
epsilon = 1e-06
axes = ("row", "col")
block_rows = 256
erf_terms = (
    -5.7109417639367166e-08,
    2.812487991832313e-06,
    -4.7398178139701486e-05,
    -5.735534068662673e-05,
    0.03636491671204567,
    0.7978729605674744,
)
nt = (((1,), (1,)), ((), ()))
tn = (((0,), (0,)), ((), ()))


def flat_index(x, y, z, core):
    return (z * 8 + (x % 2) * 4 + y) * 4 + (x // 2) * 2 + core


def pairs(dx=0, dy=0, dz=0, dc=0, by_core=False):
    found = []
    for x in range(4):
        for y in range(4):
            for z in range(4):
                for core in range(2):
                    sign = -1 if by_core and core else 1
                    target = flat_index(
                        (x + sign * dx) % 4, (y + sign * dy) % 4, (z + sign * dz) % 4, core ^ dc
                    )
                    found.append((flat_index(x, y, z, core), target))
    return found


def send(value, **hop):
    return lax.ppermute(value, axes, pairs(**hop))


def from_line(value, axis):
    return [value] + [send(value, **{axis: hop}) for hop in (1, 3, 2)]


def gelu_exact(x):
    square = jnp.minimum(x * x, 25.0)
    series = jnp.full_like(square, erf_terms[0])
    for term in erf_terms[1:]:
        series = series * square + term
    half = 0.5 * x
    return half + half * jnp.tanh(x * series)


def spot(x, y, z, core, order):
    def away(here, step):
        moved = jnp.where(step == 1, 3, jnp.where(step == 2, 1, jnp.where(step == 3, 2, 0)))
        return (here + moved) & 3

    x, y = away(x, (order >> 4) & 3), away(y, (order >> 2) & 3)
    z, core = away(z, order & 3), core ^ ((order >> 6) & 1)
    return (z * 8 + (x & 1) * 4 + y) * 4 + (x >> 1) * 2 + core


def prepare_kernel(
    lengths, tokens_ref, perm_ref, graph_ref, meta, place, packed, slot_ref, gid_ref, rows_ref, sem
):
    row, col = lax.axis_index("row"), lax.axis_index("col")
    z, y, core = row >> 3, row & 3, col & 1
    x = (col >> 1) * 2 + ((row >> 2) & 1)
    place[0] = row * 4 + col
    place[1] = row * graph_ref.shape[0]
    start = jnp.int32(0)
    for s in range(6):
        meta[s] = start
        meta[6 + s] = lengths[s]
        begin = pl.multiple_of(start, 16)
        copy = pltpu.make_async_copy(tokens_ref.at[s], packed.at[pl.ds(begin, 256)], sem)
        copy.start()
        copy.wait()
        start = start + ((lengths[s] + 15) >> 4 << 4)
    meta[12] = start
    meta[13] = (start + block_rows - 1) // block_rows
    meta[14] = 0
    meta[15] = 0

    count, texts = perm_ref.shape[1], slot_ref.shape[1]
    text = lax.broadcasted_iota(jnp.int32, (1, texts), 1)
    member = text & 7
    device = spot(x, y, z, core, text >> 3)
    tower = jnp.where(member < 6, device * 6 + member, -1)
    hit = lax.broadcasted_iota(jnp.int32, (count, texts), 0) == tower
    perm = perm_ref[...]
    high, low = (perm >> 5).astype(jnp.float32), (perm & 31).astype(jnp.float32)
    line = lax.broadcasted_iota(jnp.int32, (16, count), 0)
    digits = jnp.where(line == 0, high, jnp.where(line == 1, low, 0.0)).astype(jnp.bfloat16)
    found = jnp.dot(digits, hit.astype(jnp.bfloat16), preferred_element_type=jnp.float32)
    slot = (found[0:1] * 32.0 + found[1:2]).astype(jnp.int32)
    slot_ref[...] = jnp.where(tower >= 0, slot, -1)
    graph = lax.broadcasted_iota(jnp.int32, gid_ref.shape, 0)
    gid_ref[...] = spot(x, y, z, core, graph & 127) * 6 + (graph >> 7)

    own = graph_ref[...]
    norm = jnp.sqrt(jnp.sum(own * own, axis=-1, keepdims=True) + epsilon)
    unit = (own / norm).astype(jnp.bfloat16)
    take = lax.broadcasted_iota(jnp.int32, (16, own.shape[0]), 0) + col * 6
    take = take == lax.broadcasted_iota(jnp.int32, (16, own.shape[0]), 1)
    share = jnp.dot(take.astype(jnp.bfloat16), unit, preferred_element_type=jnp.float32)
    first = jnp.concatenate([share[k : k + 1] for k in range(4)], axis=1)
    second = jnp.concatenate([share[k : k + 1] for k in (4, 5)] * 2, axis=1)
    at = lax.broadcasted_iota(jnp.int32, rows_ref.shape, 0)
    rows_ref[...] = jnp.where(at == 6, first, jnp.where(at == 7, second, 0.0)).astype(jnp.bfloat16)


def prepare(text_hidden, lengths, perm, graph_emb):
    seqs, seq_len, width = text_hidden.shape
    count = perm.shape[0]
    smem, vmem = pl.BlockSpec(memory_space=pltpu.SMEM), pl.BlockSpec(memory_space=pltpu.VMEM)
    return pl.pallas_call(
        prepare_kernel,
        in_specs=[smem, pl.BlockSpec(memory_space=pl.ANY), vmem, vmem],
        out_specs=[smem, smem, vmem, vmem, vmem, vmem],
        out_shape=[
            jax.ShapeDtypeStruct((16,), jnp.int32),
            jax.ShapeDtypeStruct((2,), jnp.int32),
            jax.ShapeDtypeStruct((seqs * seq_len, width), jnp.bfloat16),
            jax.ShapeDtypeStruct((1, count // 6 * 8), jnp.int32),
            jax.ShapeDtypeStruct((count, 1), jnp.int32),
            jax.ShapeDtypeStruct((8, width), jnp.bfloat16),
        ],
        scratch_shapes=[pltpu.SemaphoreType.DMA],
        compiler_params=pltpu.CompilerParams(vmem_limit_bytes=12 * 2**20),
    )(lengths, text_hidden, perm.reshape(1, count), graph_emb)


def merge_bias(tiles, run, at=0):
    lane = lax.broadcasted_iota(jnp.int32, (1, tiles[0].shape[1]), 1) // run % 4
    row = tiles[0].astype(jnp.float32)[at : at + 1]
    for k in range(1, 4):
        row = jnp.where(lane == k, tiles[k].astype(jnp.float32)[at : at + 1], row)
    return jnp.broadcast_to(row, tiles[0].shape).astype(jnp.bfloat16)


def split_kernel(*refs):
    parts = refs[:4]
    for k, out in enumerate(refs[-2:]):
        for s, part in enumerate(parts):
            out[16 * s : 16 * s + 16, :] = part[16 * k : 16 * k + 16, :]
            out[64 + 16 * s : 80 + 16 * s, :] = part[32 + 16 * k : 48 + 16 * k, :]
        out[128:144, :] = merge_bias([p[64:80, :] for p in parts], 16, 8 * k)


def join_kernel(*refs):
    for k, out in enumerate(refs[-2:]):
        parts = refs[4 * k : 4 * k + 4]
        for s, part in enumerate(parts):
            out[64 * s : 64 * s + 64, :] = part[0:64, :]
            out[256 + 64 * s : 320 + 64 * s, :] = part[64:128, :]
        out[512:528, :] = merge_bias([p[128:144, :] for p in parts], 64)


def arrange(body, parts, rows, done=()):
    shape = jax.ShapeDtypeStruct((rows, parts[0].shape[1]), jnp.bfloat16)
    return pl.pallas_call(
        body,
        in_specs=[pl.BlockSpec(memory_space=pltpu.VMEM)] * len(parts)
        + [pl.BlockSpec(memory_space=pl.ANY)] * len(done),
        out_specs=[pl.BlockSpec(memory_space=pltpu.VMEM)] * 2,
        out_shape=[shape, shape],
        compiler_params=pltpu.CompilerParams(vmem_limit_bytes=4 * 2**20),
    )(*parts, *done)


def ffn_tiles(x, weights):
    up = jnp.concatenate([w[0:256, :] for w in weights], axis=0)
    down = jnp.concatenate([w[256:512, :] for w in weights], axis=0)
    bias = jnp.concatenate(
        [w[512:528, 0:256].astype(jnp.float32)[0:1] for w in weights], axis=1
    )
    rows = x.shape[0]
    halves = [x] if rows == block_rows else [x[: rows // 2], x[rows // 2 :]]
    preact = [
        lax.dot_general(h, up, nt, preferred_element_type=jnp.float32) + bias for h in halves
    ]
    parts = [
        jnp.dot(gelu_exact(p).astype(jnp.bfloat16), down, preferred_element_type=jnp.float32)
        for p in preact
    ]
    return jnp.concatenate(parts, axis=0)


def ffn_kernel(count, first, last, meta, x_ref, *refs):
    weights, refs = refs[:count], refs[count:]
    if not first:
        acc_in, refs = refs[0], refs[1:]
    if last:
        gain_ref, graph_ref, pooled_ref, sums = refs
        sums[...] = jnp.zeros_like(sums)
    else:
        out_ref, token_ref = refs
        token_ref[...] = jnp.zeros_like(token_ref)

    def rows_step(base, height):
        at = pl.ds(pl.multiple_of(base, block_rows), height)
        x = x_ref[at, :]
        total = ffn_tiles(x, weights)
        if not first:
            total = acc_in[at, :] + total
        if not last:
            out_ref[at, :] = total
            return
        summed = x.astype(jnp.float32) + total
        centre = summed - jnp.mean(summed, axis=-1, keepdims=True)
        spread = jnp.mean(centre * centre, axis=-1, keepdims=True)
        normed = centre * lax.rsqrt(spread + epsilon) * gain_ref[...]
        row = base + lax.broadcasted_iota(jnp.int32, (height, 1), 0)
        groups = height // 16
        group = base + 16 * lax.broadcasted_iota(jnp.int32, (8, groups), 1)
        seq = lax.broadcasted_iota(jnp.int32, (8, groups), 0)
        valid = row < 0
        member = group < 0
        for s in range(6):
            start, stop = meta[s], meta[s] + meta[6 + s]
            valid |= (row >= start) & (row < stop)
            member |= (group >= start) & (group < stop) & (seq == s)
        normed = jnp.where(valid, normed, 0.0)
        partial = jnp.sum(normed.reshape(groups, 16, normed.shape[1]), axis=1)
        sums[...] += jnp.dot(
            member.astype(jnp.float32),
            partial,
            precision=lax.Precision.HIGHEST,
            preferred_element_type=jnp.float32,
        )

    blocks = meta[13]
    double = 2 * block_rows

    @pl.loop(0, blocks // 2)
    def _(i):
        rows_step(i * double, double)

    @pl.when(blocks % 2 == 1)
    def _():
        rows_step((blocks - 1) * block_rows, block_rows)

    if last:
        seq = lax.broadcasted_iota(jnp.int32, (8, 1), 0)
        tokens = jnp.ones((8, 1), jnp.float32)
        for s in range(6):
            tokens = jnp.where(seq == s, meta[6 + s].astype(jnp.float32), tokens)
        means = (sums[...] / tokens).astype(jnp.bfloat16)
        pooled_ref[...] = jnp.where(seq < 6, means, graph_ref[...])


def ffn_step(meta, packed, weights, acc=None, gain=None, graph_rows=None):
    rows, width = packed.shape
    count, first, last = len(weights), acc is None, gain is not None
    operands = [packed, *weights]
    aliases = {}
    if not first:
        if not last:
            aliases = {1 + len(operands): 0}
        operands.append(acc)
    scratch = []
    if last:
        operands += [gain, graph_rows]
        out_shape = jax.ShapeDtypeStruct((8, width), jnp.bfloat16)
        scratch = [pltpu.VMEM((8, width), jnp.float32)]
    else:
        out_shape = [jax.ShapeDtypeStruct((rows, width), jnp.float32)]
        out_shape.append(jax.ShapeDtypeStruct((8, 128), jnp.float32))
    vmem = pl.BlockSpec(memory_space=pltpu.VMEM)
    return pl.pallas_call(
        functools.partial(ffn_kernel, count, first, last),
        in_specs=[pl.BlockSpec(memory_space=pltpu.SMEM)]
        + [pl.BlockSpec(memory_space=pltpu.VMEM)] * len(operands),
        out_specs=vmem if last else [vmem, vmem],
        scratch_shapes=scratch,
        out_shape=out_shape,
        input_output_aliases=aliases,
        compiler_params=pltpu.CompilerParams(vmem_limit_bytes=8 * 2**20),
        cost_estimate=pl.CostEstimate(
            flops=4 * rows * 256 * count * width, bytes_accessed=2**20, transcendentals=0
        ),
    )(meta, *operands)


def tie_kernel(*refs):
    del refs


def after(values, done):
    return pl.pallas_call(
        tie_kernel,
        in_specs=[pl.BlockSpec(memory_space=pl.ANY)] * (len(values) + 1),
        out_specs=[pl.BlockSpec(memory_space=pl.ANY)] * len(values),
        out_shape=[jax.ShapeDtypeStruct(v.shape, v.dtype) for v in values],
        input_output_aliases={k: k for k in range(len(values))},
        compiler_params=pltpu.CompilerParams(vmem_limit_bytes=2**20),
    )(*values, done)


def tail_kernel(place, *refs):
    pieces, refs = refs[:8], refs[8:]
    proj_ref, own_ref, slot_ref, gid_ref = refs[:4]
    loss_ref, grad_graph_ref, grad_text_ref, grad_proj_ref = refs[4:]
    flat, row_first = place[0], place[1]
    pooled = jnp.concatenate([p[...] for p in pieces], axis=0)
    texts = pooled.shape[0]
    graphs = gid_ref.shape[0]
    devices = texts // 8
    text_emb = jnp.dot(pooled, proj_ref[...], preferred_element_type=jnp.float32)
    text_norm = jnp.sqrt(jnp.sum(text_emb * text_emb, axis=-1, keepdims=True) + epsilon)
    text_unit = text_emb / text_norm
    text_send = text_unit.astype(jnp.bfloat16)
    line = lax.broadcasted_iota(jnp.int32, (2 * devices, texts), 0)
    wanted = jnp.where(line < devices, 8 * line + 6, 8 * (line - devices) + 7)
    carried = wanted == lax.broadcasted_iota(jnp.int32, (2 * devices, texts), 1)
    carriers = jnp.dot(
        carried.astype(jnp.bfloat16), pooled, preferred_element_type=jnp.float32
    ).astype(jnp.bfloat16)
    graph_send = jnp.concatenate(
        [carriers[0:devices, 256 * k : 256 * k + 256] for k in range(4)]
        + [carriers[devices:, 256 * k : 256 * k + 256] for k in range(2)],
        axis=0,
    )
    slot = slot_ref[...]
    valid = slot >= 0

    def scores(rows_send):
        logits = (
            lax.dot_general(rows_send, text_send, nt, preferred_element_type=jnp.float32)
            * sharpness
        )
        expo = jnp.where(valid, jnp.exp(logits), 0.0)
        return logits, expo, jnp.sum(expo, axis=1, keepdims=True)

    logits, expo, row_total = scores(graph_send)
    col_total = jnp.where(valid, jnp.sum(expo, axis=0, keepdims=True), 1.0)
    col_scale = 0.5 / col_total
    matched = gid_ref[...] == slot
    diagonal = jnp.sum(jnp.where(matched, logits, 0.0), axis=1, keepdims=True)
    row_terms = jnp.sum(jnp.log(row_total) - 2.0 * diagonal, axis=0, keepdims=True)
    col_terms = jnp.sum(jnp.log(col_total), axis=1, keepdims=True)
    loss_ref[...] = (row_terms + col_terms) / (2.0 * graphs)

    def weigh(expo, row_total, matched):
        weights = expo * (0.5 / row_total) + expo * col_scale
        return (weights - jnp.where(matched, 1.0, 0.0)).astype(jnp.bfloat16)

    weights = weigh(expo, row_total, matched)
    text_grad = (
        lax.dot_general(weights, graph_send, tn, preferred_element_type=jnp.float32)
        * sharpness
    )
    along = jnp.sum(text_unit * text_grad, axis=-1, keepdims=True)
    grad_text = (text_grad - text_unit * along) / text_norm
    grad_text_ref[...] = grad_text[0:8]

    own = own_ref[...]
    own_norm = jnp.sqrt(jnp.sum(own * own, axis=-1, keepdims=True) + epsilon)
    own_unit = own / own_norm
    _, own_expo, own_total = scores(own_unit.astype(jnp.bfloat16))
    own_rows = own.shape[0]
    own_matched = row_first + lax.broadcasted_iota(jnp.int32, (own_rows, texts), 0) == slot
    own_weights = weigh(own_expo, own_total, own_matched)
    graph_grad = (
        jnp.dot(own_weights, text_send, preferred_element_type=jnp.float32) * sharpness
    )
    own_along = jnp.sum(own_unit * graph_grad, axis=-1, keepdims=True)
    grad_graph_ref[...] = (graph_grad - own_unit * own_along) / own_norm

    width = pooled.shape[1]
    feature = lax.broadcasted_iota(jnp.int32, (width, 128), 0)
    wanted = flat * 8 + lax.broadcasted_iota(jnp.int32, (width, 128), 1)
    pick = (feature == wanted).astype(jnp.bfloat16)
    picked = jnp.dot(pooled, pick, preferred_element_type=jnp.float32)
    grad_proj = lax.dot_general(
        picked,
        grad_text,
        tn,
        precision=lax.Precision.HIGHEST,
        preferred_element_type=jnp.float32,
    )
    grad_proj_ref[...] = grad_proj[0:8]


def tail(place, pieces, proj_weight, graph_emb, slot, gid):
    shapes = [(1, 1), graph_emb.shape, (8, 256), (8, 256)]
    return pl.pallas_call(
        tail_kernel,
        in_specs=[pl.BlockSpec(memory_space=pltpu.SMEM)]
        + [pl.BlockSpec(memory_space=pltpu.VMEM)] * 12,
        out_specs=[pl.BlockSpec(memory_space=pltpu.VMEM)] * 4,
        out_shape=[jax.ShapeDtypeStruct(s, jnp.float32) for s in shapes],
        compiler_params=pltpu.CompilerParams(vmem_limit_bytes=48 * 2**20),
    )(place, *pieces, proj_weight, graph_emb, slot, gid)


def gather_weights(up_weight, up_bias, down_weight, done):
    width = up_weight.shape[1]
    bias = [jnp.tile(b.reshape(1, 16), (8, width // 16)) for b in (up_bias[:16], up_bias[16:])]
    own = jnp.concatenate([up_weight, down_weight, *bias], axis=0)
    halves = arrange(split_kernel, from_line(own, "dz"), 144)
    pieces = []
    for half, inner in zip(halves, ("dx", "dy")):
        ring = [half]
        for _ in range(3):
            ring.append(send(ring[-1], by_core=True, **{inner: 1}))
        pieces += ring
    return arrange(join_kernel, pieces, 528, (done,))


def shards(
    text_hidden, lengths, up_weight, up_bias, down_weight, ln_gain, proj_weight, graph_emb, perm
):
    meta, place, packed, slot, gid, graph_rows = prepare(text_hidden, lengths, perm, graph_emb)
    mine = gather_weights(up_weight, up_bias, down_weight, graph_rows)
    step = functools.partial(ffn_step, meta, packed)
    acc = None
    for turn in range(4):
        other = [send(block, dc=1) for block in mine]
        if turn < 3:
            coming = [
                send(block, by_core=True, **{outer: 1}) for block, outer in zip(mine, ("dy", "dx"))
            ]
        acc, _ = step(mine, acc)
        if turn < 3:
            acc, token = step(other, acc)
            mine = after(coming, token)
    pooled = step(other, acc, ln_gain.reshape(1, -1), graph_rows)
    for axis in ("dz", "dy"):
        pooled = jnp.concatenate(from_line(pooled, axis), axis=0)
    line = from_line(pooled, "dx")
    pieces = line + [send(value, dc=1) for value in line]

    loss, grad_graph, grad_text, grad_proj = tail(
        place, pieces, proj_weight, graph_emb, slot, gid
    )
    return (loss[0, 0], grad_graph, grad_text[:6], grad_proj)


def solution(mesh):
    return jax.shard_map(
        shards,
        mesh=mesh,
        in_specs=(
            P(("row", "col"), None, None),
            P(("row", "col")),
            P(("row", "col"), None),
            P(("row", "col")),
            P(("row", "col"), None),
            P(),
            P(),
            P("row", None),
            P(),
        ),
        out_specs=(P(), P("row", None), P(("row", "col"), None), P(("row", "col"), None)),
        check_vma=False,
    )
```

```python
import functools

import jax
import jax.numpy as jnp
from jax import lax
from jax.experimental import pallas as pl
from jax.experimental.pallas import tpu as pltpu
from jax.sharding import PartitionSpec as P

sharpness = 1.0 / 0.02
epsilon = 1e-06
axes = ("row", "col")
block_rows = 256
erf_terms = (
    -5.7109417639367166e-08,
    2.812487991832313e-06,
    -4.7398178139701486e-05,
    -5.735534068662673e-05,
    0.03636491671204567,
    0.7978729605674744,
)
nt = (((1,), (1,)), ((), ()))
tn = (((0,), (0,)), ((), ()))


def flat_index(x, y, z, core):
    return (z * 8 + (x % 2) * 4 + y) * 4 + (x // 2) * 2 + core


def pairs(dx=0, dy=0, dz=0, dc=0, by_core=False):
    found = []
    for x in range(4):
        for y in range(4):
            for z in range(4):
                for core in range(2):
                    sign = -1 if by_core and core else 1
                    target = flat_index(
                        (x + sign * dx) % 4, (y + sign * dy) % 4, (z + sign * dz) % 4, core ^ dc
                    )
                    found.append((flat_index(x, y, z, core), target))
    return found


def send(value, **hop):
    return lax.ppermute(value, axes, pairs(**hop))


def from_line(value, axis):
    return [value] + [send(value, **{axis: hop}) for hop in (1, 3, 2)]


def gelu_exact(x):
    square = jnp.minimum(x * x, 25.0)
    series = jnp.full_like(square, erf_terms[0])
    for term in erf_terms[1:]:
        series = series * square + term
    half = 0.5 * x
    return half + half * jnp.tanh(x * series)


def spot(x, y, z, core, order):
    def away(here, step):
        moved = jnp.where(step == 1, 3, jnp.where(step == 2, 1, jnp.where(step == 3, 2, 0)))
        return (here + moved) & 3

    x, y = away(x, (order >> 4) & 3), away(y, (order >> 2) & 3)
    z, core = away(z, order & 3), core ^ ((order >> 6) & 1)
    return (z * 8 + (x & 1) * 4 + y) * 4 + (x >> 1) * 2 + core


def prepare_kernel(
    lengths, tokens_ref, perm_ref, graph_ref, meta, place, packed, slot_ref, gid_ref, rows_ref, sem
):
    row, col = lax.axis_index("row"), lax.axis_index("col")
    z, y, core = row >> 3, row & 3, col & 1
    x = (col >> 1) * 2 + ((row >> 2) & 1)
    place[0] = row * 4 + col
    place[1] = row * graph_ref.shape[0]
    start = jnp.int32(0)
    for s in range(6):
        meta[s] = start
        meta[6 + s] = lengths[s]
        begin = pl.multiple_of(start, 16)
        copy = pltpu.make_async_copy(tokens_ref.at[s], packed.at[pl.ds(begin, 256)], sem)
        copy.start()
        copy.wait()
        start = start + ((lengths[s] + 15) >> 4 << 4)
    meta[12] = start
    meta[13] = (start + block_rows - 1) // block_rows
    meta[14] = 0
    meta[15] = 0

    count, texts = perm_ref.shape[1], slot_ref.shape[1]
    text = lax.broadcasted_iota(jnp.int32, (1, texts), 1)
    member = text & 7
    device = spot(x, y, z, core, text >> 3)
    tower = jnp.where(member < 6, device * 6 + member, -1)
    hit = lax.broadcasted_iota(jnp.int32, (count, texts), 0) == tower
    perm = perm_ref[...]
    high, low = (perm >> 5).astype(jnp.float32), (perm & 31).astype(jnp.float32)
    line = lax.broadcasted_iota(jnp.int32, (16, count), 0)
    digits = jnp.where(line == 0, high, jnp.where(line == 1, low, 0.0)).astype(jnp.bfloat16)
    found = jnp.dot(digits, hit.astype(jnp.bfloat16), preferred_element_type=jnp.float32)
    slot = (found[0:1] * 32.0 + found[1:2]).astype(jnp.int32)
    slot_ref[...] = jnp.where(tower >= 0, slot, -1)
    graph = lax.broadcasted_iota(jnp.int32, gid_ref.shape, 0)
    gid_ref[...] = spot(x, y, z, core, graph & 127) * 6 + (graph >> 7)

    own = graph_ref[...]
    norm = jnp.sqrt(jnp.sum(own * own, axis=-1, keepdims=True) + epsilon)
    unit = (own / norm).astype(jnp.bfloat16)
    take = lax.broadcasted_iota(jnp.int32, (16, own.shape[0]), 0) + col * 6
    take = take == lax.broadcasted_iota(jnp.int32, (16, own.shape[0]), 1)
    share = jnp.dot(take.astype(jnp.bfloat16), unit, preferred_element_type=jnp.float32)
    first = jnp.concatenate([share[k : k + 1] for k in range(4)], axis=1)
    second = jnp.concatenate([share[k : k + 1] for k in (4, 5)] * 2, axis=1)
    at = lax.broadcasted_iota(jnp.int32, rows_ref.shape, 0)
    rows_ref[...] = jnp.where(at == 6, first, jnp.where(at == 7, second, 0.0)).astype(jnp.bfloat16)


def prepare(text_hidden, lengths, perm, graph_emb):
    seqs, seq_len, width = text_hidden.shape
    count = perm.shape[0]
    smem, vmem = pl.BlockSpec(memory_space=pltpu.SMEM), pl.BlockSpec(memory_space=pltpu.VMEM)
    return pl.pallas_call(
        prepare_kernel,
        in_specs=[smem, pl.BlockSpec(memory_space=pl.ANY), vmem, vmem],
        out_specs=[smem, smem, vmem, vmem, vmem, vmem],
        out_shape=[
            jax.ShapeDtypeStruct((16,), jnp.int32),
            jax.ShapeDtypeStruct((2,), jnp.int32),
            jax.ShapeDtypeStruct((seqs * seq_len, width), jnp.bfloat16),
            jax.ShapeDtypeStruct((1, count // 6 * 8), jnp.int32),
            jax.ShapeDtypeStruct((count, 1), jnp.int32),
            jax.ShapeDtypeStruct((8, width), jnp.bfloat16),
        ],
        scratch_shapes=[pltpu.SemaphoreType.DMA],
        compiler_params=pltpu.CompilerParams(vmem_limit_bytes=12 * 2**20),
    )(lengths, text_hidden, perm.reshape(1, count), graph_emb)


def merge_bias(tiles, run, at=0):
    lane = lax.broadcasted_iota(jnp.int32, (1, tiles[0].shape[1]), 1) // run % 4
    row = tiles[0].astype(jnp.float32)[at : at + 1]
    for k in range(1, 4):
        row = jnp.where(lane == k, tiles[k].astype(jnp.float32)[at : at + 1], row)
    return jnp.broadcast_to(row, tiles[0].shape).astype(jnp.bfloat16)


def split_kernel(*refs):
    parts = refs[:4]
    for k, out in enumerate(refs[-2:]):
        for s, part in enumerate(parts):
            out[16 * s : 16 * s + 16, :] = part[16 * k : 16 * k + 16, :]
            out[64 + 16 * s : 80 + 16 * s, :] = part[32 + 16 * k : 48 + 16 * k, :]
        out[128:144, :] = merge_bias([p[64:80, :] for p in parts], 16, 8 * k)


def join_kernel(*refs):
    for k, out in enumerate(refs[-2:]):
        parts = refs[4 * k : 4 * k + 4]
        for s, part in enumerate(parts):
            out[64 * s : 64 * s + 64, :] = part[0:64, :]
            out[256 + 64 * s : 320 + 64 * s, :] = part[64:128, :]
        out[512:528, :] = merge_bias([p[128:144, :] for p in parts], 64)


def arrange(body, parts, rows, done=()):
    shape = jax.ShapeDtypeStruct((rows, parts[0].shape[1]), jnp.bfloat16)
    return pl.pallas_call(
        body,
        in_specs=[pl.BlockSpec(memory_space=pltpu.VMEM)] * len(parts)
        + [pl.BlockSpec(memory_space=pl.ANY)] * len(done),
        out_specs=[pl.BlockSpec(memory_space=pltpu.VMEM)] * 2,
        out_shape=[shape, shape],
        compiler_params=pltpu.CompilerParams(vmem_limit_bytes=4 * 2**20),
    )(*parts, *done)


def ffn_tiles(x, weights):
    up = jnp.concatenate([w[0:256, :] for w in weights], axis=0)
    down = jnp.concatenate([w[256:512, :] for w in weights], axis=0)
    bias = jnp.concatenate(
        [w[512:528, 0:256].astype(jnp.float32)[0:1] for w in weights], axis=1
    )
    rows = x.shape[0]
    halves = [x] if rows == block_rows else [x[: rows // 2], x[rows // 2 :]]
    preact = [
        lax.dot_general(h, up, nt, preferred_element_type=jnp.float32) + bias for h in halves
    ]
    parts = [
        jnp.dot(gelu_exact(p).astype(jnp.bfloat16), down, preferred_element_type=jnp.float32)
        for p in preact
    ]
    return jnp.concatenate(parts, axis=0)


def ffn_kernel(count, first, last, meta, x_ref, *refs):
    weights, refs = refs[:count], refs[count:]
    if not first:
        acc_in, refs = refs[0], refs[1:]
    if last:
        gain_ref, graph_ref, pooled_ref, sums = refs
        sums[...] = jnp.zeros_like(sums)
    else:
        out_ref, token_ref = refs
        token_ref[...] = jnp.zeros_like(token_ref)

    def rows_step(base, height):
        at = pl.ds(pl.multiple_of(base, block_rows), height)
        x = x_ref[at, :]
        total = ffn_tiles(x, weights)
        if not first:
            total = acc_in[at, :] + total
        if not last:
            out_ref[at, :] = total
            return
        summed = x.astype(jnp.float32) + total
        centre = summed - jnp.mean(summed, axis=-1, keepdims=True)
        spread = jnp.mean(centre * centre, axis=-1, keepdims=True)
        normed = centre * lax.rsqrt(spread + epsilon) * gain_ref[...]
        row = base + lax.broadcasted_iota(jnp.int32, (height, 1), 0)
        groups = height // 16
        group = base + 16 * lax.broadcasted_iota(jnp.int32, (8, groups), 1)
        seq = lax.broadcasted_iota(jnp.int32, (8, groups), 0)
        valid = row < 0
        member = group < 0
        for s in range(6):
            start, stop = meta[s], meta[s] + meta[6 + s]
            valid |= (row >= start) & (row < stop)
            member |= (group >= start) & (group < stop) & (seq == s)
        normed = jnp.where(valid, normed, 0.0)
        partial = jnp.sum(normed.reshape(groups, 16, normed.shape[1]), axis=1)
        sums[...] += jnp.dot(
            member.astype(jnp.float32),
            partial,
            precision=lax.Precision.HIGHEST,
            preferred_element_type=jnp.float32,
        )

    blocks = meta[13]
    double = 2 * block_rows

    @pl.loop(0, blocks // 2)
    def _(i):
        rows_step(i * double, double)

    @pl.when(blocks % 2 == 1)
    def _():
        rows_step((blocks - 1) * block_rows, block_rows)

    if last:
        seq = lax.broadcasted_iota(jnp.int32, (8, 1), 0)
        tokens = jnp.ones((8, 1), jnp.float32)
        for s in range(6):
            tokens = jnp.where(seq == s, meta[6 + s].astype(jnp.float32), tokens)
        means = (sums[...] / tokens).astype(jnp.bfloat16)
        pooled_ref[...] = jnp.where(seq < 6, means, graph_ref[...])


def ffn_step(meta, packed, weights, acc=None, gain=None, graph_rows=None):
    rows, width = packed.shape
    count, first, last = len(weights), acc is None, gain is not None
    operands = [packed, *weights]
    aliases = {}
    if not first:
        if not last:
            aliases = {1 + len(operands): 0}
        operands.append(acc)
    scratch = []
    if last:
        operands += [gain, graph_rows]
        out_shape = jax.ShapeDtypeStruct((8, width), jnp.bfloat16)
        scratch = [pltpu.VMEM((8, width), jnp.float32)]
    else:
        out_shape = [jax.ShapeDtypeStruct((rows, width), jnp.float32)]
        out_shape.append(jax.ShapeDtypeStruct((8, 128), jnp.float32))
    vmem = pl.BlockSpec(memory_space=pltpu.VMEM)
    return pl.pallas_call(
        functools.partial(ffn_kernel, count, first, last),
        in_specs=[pl.BlockSpec(memory_space=pltpu.SMEM)]
        + [pl.BlockSpec(memory_space=pltpu.VMEM)] * len(operands),
        out_specs=vmem if last else [vmem, vmem],
        scratch_shapes=scratch,
        out_shape=out_shape,
        input_output_aliases=aliases,
        compiler_params=pltpu.CompilerParams(vmem_limit_bytes=8 * 2**20),
        cost_estimate=pl.CostEstimate(
            flops=4 * rows * 256 * count * width, bytes_accessed=2**20, transcendentals=0
        ),
    )(meta, *operands)


def tie_kernel(*refs):
    del refs


def after(values, done):
    return pl.pallas_call(
        tie_kernel,
        in_specs=[pl.BlockSpec(memory_space=pl.ANY)] * (len(values) + 1),
        out_specs=[pl.BlockSpec(memory_space=pl.ANY)] * len(values),
        out_shape=[jax.ShapeDtypeStruct(v.shape, v.dtype) for v in values],
        input_output_aliases={k: k for k in range(len(values))},
        compiler_params=pltpu.CompilerParams(vmem_limit_bytes=2**20),
    )(*values, done)


def tail_kernel(place, *refs):
    pieces, refs = refs[:8], refs[8:]
    proj_ref, own_ref, slot_ref, gid_ref = refs[:4]
    loss_ref, grad_graph_ref, grad_text_ref, grad_proj_ref = refs[4:]
    flat, row_first = place[0], place[1]
    pooled = jnp.concatenate([p[...] for p in pieces], axis=0)
    texts = pooled.shape[0]
    graphs = gid_ref.shape[0]
    devices = texts // 8
    text_emb = jnp.dot(pooled, proj_ref[...], preferred_element_type=jnp.float32)
    text_norm = jnp.sqrt(jnp.sum(text_emb * text_emb, axis=-1, keepdims=True) + epsilon)
    text_unit = text_emb / text_norm
    text_send = text_unit.astype(jnp.bfloat16)
    line = lax.broadcasted_iota(jnp.int32, (2 * devices, texts), 0)
    wanted = jnp.where(line < devices, 8 * line + 6, 8 * (line - devices) + 7)
    carried = wanted == lax.broadcasted_iota(jnp.int32, (2 * devices, texts), 1)
    carriers = jnp.dot(
        carried.astype(jnp.bfloat16), pooled, preferred_element_type=jnp.float32
    ).astype(jnp.bfloat16)
    graph_send = jnp.concatenate(
        [carriers[0:devices, 256 * k : 256 * k + 256] for k in range(4)]
        + [carriers[devices:, 256 * k : 256 * k + 256] for k in range(2)],
        axis=0,
    )
    slot = slot_ref[...]
    valid = slot >= 0

    def scores(rows_send):
        logits = (
            lax.dot_general(rows_send, text_send, nt, preferred_element_type=jnp.float32)
            * sharpness
        )
        expo = jnp.where(valid, jnp.exp(logits), 0.0)
        return logits, expo, jnp.sum(expo, axis=1, keepdims=True)

    logits, expo, row_total = scores(graph_send)
    col_total = jnp.where(valid, jnp.sum(expo, axis=0, keepdims=True), 1.0)
    col_scale = 0.5 / col_total
    matched = gid_ref[...] == slot
    diagonal = jnp.sum(jnp.where(matched, logits, 0.0), axis=1, keepdims=True)
    row_terms = jnp.sum(jnp.log(row_total) - 2.0 * diagonal, axis=0, keepdims=True)
    col_terms = jnp.sum(jnp.log(col_total), axis=1, keepdims=True)
    loss_ref[...] = (row_terms + col_terms) / (2.0 * graphs)

    def weigh(expo, row_total, matched):
        weights = expo * (0.5 / row_total) + expo * col_scale
        return (weights - jnp.where(matched, 1.0, 0.0)).astype(jnp.bfloat16)

    weights = weigh(expo, row_total, matched)
    text_grad = (
        lax.dot_general(weights, graph_send, tn, preferred_element_type=jnp.float32)
        * sharpness
    )
    along = jnp.sum(text_unit * text_grad, axis=-1, keepdims=True)
    grad_text = (text_grad - text_unit * along) / text_norm
    grad_text_ref[...] = grad_text[0:8]

    own = own_ref[...]
    own_norm = jnp.sqrt(jnp.sum(own * own, axis=-1, keepdims=True) + epsilon)
    own_unit = own / own_norm
    _, own_expo, own_total = scores(own_unit.astype(jnp.bfloat16))
    own_rows = own.shape[0]
    own_matched = row_first + lax.broadcasted_iota(jnp.int32, (own_rows, texts), 0) == slot
    own_weights = weigh(own_expo, own_total, own_matched)
    graph_grad = (
        jnp.dot(own_weights, text_send, preferred_element_type=jnp.float32) * sharpness
    )
    own_along = jnp.sum(own_unit * graph_grad, axis=-1, keepdims=True)
    grad_graph_ref[...] = (graph_grad - own_unit * own_along) / own_norm

    width = pooled.shape[1]
    feature = lax.broadcasted_iota(jnp.int32, (width, 128), 0)
    wanted = flat * 8 + lax.broadcasted_iota(jnp.int32, (width, 128), 1)
    pick = (feature == wanted).astype(jnp.bfloat16)
    picked = jnp.dot(pooled, pick, preferred_element_type=jnp.float32)
    grad_proj = lax.dot_general(
        picked,
        grad_text,
        tn,
        precision=lax.Precision.HIGHEST,
        preferred_element_type=jnp.float32,
    )
    grad_proj_ref[...] = grad_proj[0:8]


def tail(place, pieces, proj_weight, graph_emb, slot, gid):
    shapes = [(1, 1), graph_emb.shape, (8, 256), (8, 256)]
    return pl.pallas_call(
        tail_kernel,
        in_specs=[pl.BlockSpec(memory_space=pltpu.SMEM)]
        + [pl.BlockSpec(memory_space=pltpu.VMEM)] * 12,
        out_specs=[pl.BlockSpec(memory_space=pltpu.VMEM)] * 4,
        out_shape=[jax.ShapeDtypeStruct(s, jnp.float32) for s in shapes],
        compiler_params=pltpu.CompilerParams(vmem_limit_bytes=48 * 2**20),
    )(place, *pieces, proj_weight, graph_emb, slot, gid)


def gather_weights(up_weight, up_bias, down_weight, done):
    width = up_weight.shape[1]
    bias = [jnp.tile(b.reshape(1, 16), (8, width // 16)) for b in (up_bias[:16], up_bias[16:])]
    own = jnp.concatenate([up_weight, down_weight, *bias], axis=0)
    halves = arrange(split_kernel, from_line(own, "dz"), 144)
    pieces = []
    for half, inner in zip(halves, ("dx", "dy")):
        ahead, behind = (send(half, by_core=True, **{inner: hop}) for hop in (1, 3))
        pieces += [half, ahead, send(ahead, by_core=True, **{inner: 1}), behind]
    return arrange(join_kernel, pieces, 528, (done,))


def shards(
    text_hidden, lengths, up_weight, up_bias, down_weight, ln_gain, proj_weight, graph_emb, perm
):
    meta, place, packed, slot, gid, graph_rows = prepare(text_hidden, lengths, perm, graph_emb)
    mine = gather_weights(up_weight, up_bias, down_weight, graph_rows)
    step = functools.partial(ffn_step, meta, packed)
    acc = None
    for turn in range(4):
        other = [send(block, dc=1) for block in mine]
        if turn < 3:
            coming = [
                send(block, by_core=True, **{outer: 1}) for block, outer in zip(mine, ("dy", "dx"))
            ]
        acc, _ = step(mine, acc)
        if turn < 3:
            acc, token = step(other, acc)
            mine = after(coming, token)
    pooled = step(other, acc, ln_gain.reshape(1, -1), graph_rows)
    for axis in ("dz", "dy"):
        pooled = jnp.concatenate(from_line(pooled, axis), axis=0)
    line = from_line(pooled, "dx")
    pieces = line + [send(value, dc=1) for value in line]

    loss, grad_graph, grad_text, grad_proj = tail(
        place, pieces, proj_weight, graph_emb, slot, gid
    )
    return (loss[0, 0], grad_graph, grad_text[:6], grad_proj)


def solution(mesh):
    return jax.shard_map(
        shards,
        mesh=mesh,
        in_specs=(
            P(("row", "col"), None, None),
            P(("row", "col")),
            P(("row", "col"), None),
            P(("row", "col")),
            P(("row", "col"), None),
            P(),
            P(),
            P("row", None),
            P(),
        ),
        out_specs=(P(), P("row", None), P(("row", "col"), None), P(("row", "col"), None)),
        check_vma=False,
    )
```

```python
import functools

import jax
import jax.numpy as jnp
from jax import lax
from jax.experimental import pallas as pl
from jax.experimental.pallas import tpu as pltpu
from jax.sharding import PartitionSpec as P

sharpness = 1.0 / 0.02
epsilon = 1e-06
axes = ("row", "col")
block_rows = 256
erf_terms = (
    -5.7109417639367166e-08,
    2.812487991832313e-06,
    -4.7398178139701486e-05,
    -5.735534068662673e-05,
    0.03636491671204567,
    0.7978729605674744,
)
nt = (((1,), (1,)), ((), ()))
tn = (((0,), (0,)), ((), ()))


def flat_index(x, y, z, core):
    return (z * 8 + (x % 2) * 4 + y) * 4 + (x // 2) * 2 + core


def pairs(dx=0, dy=0, dz=0, dc=0, by_core=False):
    found = []
    for x in range(4):
        for y in range(4):
            for z in range(4):
                for core in range(2):
                    sign = -1 if by_core and core else 1
                    target = flat_index(
                        (x + sign * dx) % 4, (y + sign * dy) % 4, (z + sign * dz) % 4, core ^ dc
                    )
                    found.append((flat_index(x, y, z, core), target))
    return found


def send(value, **hop):
    return lax.ppermute(value, axes, pairs(**hop))


def from_line(value, axis):
    return [value] + [send(value, **{axis: hop}) for hop in (1, 3, 2)]


def gelu_exact(x):
    square = jnp.minimum(x * x, 25.0)
    series = jnp.full_like(square, erf_terms[0])
    for term in erf_terms[1:]:
        series = series * square + term
    half = 0.5 * x
    return half + half * jnp.tanh(x * series)


def spot(x, y, z, core, order):
    def away(here, step):
        moved = jnp.where(step == 1, 3, jnp.where(step == 2, 1, jnp.where(step == 3, 2, 0)))
        return (here + moved) & 3

    x, y = away(x, (order >> 4) & 3), away(y, (order >> 2) & 3)
    z, core = away(z, order & 3), core ^ ((order >> 6) & 1)
    return (z * 8 + (x & 1) * 4 + y) * 4 + (x >> 1) * 2 + core


def prepare_kernel(
    lengths, tokens_ref, perm_ref, graph_ref, meta, place, packed, slot_ref, gid_ref, rows_ref, sem
):
    row, col = lax.axis_index("row"), lax.axis_index("col")
    z, y, core = row >> 3, row & 3, col & 1
    x = (col >> 1) * 2 + ((row >> 2) & 1)
    place[0] = row * 4 + col
    place[1] = row * graph_ref.shape[0]
    start = jnp.int32(0)
    for s in range(6):
        meta[s] = start
        meta[6 + s] = lengths[s]
        begin = pl.multiple_of(start, 16)
        copy = pltpu.make_async_copy(tokens_ref.at[s], packed.at[pl.ds(begin, 256)], sem)
        copy.start()
        copy.wait()
        start = start + ((lengths[s] + 15) >> 4 << 4)
    meta[12] = start
    meta[13] = (start + block_rows - 1) // block_rows
    meta[14] = 0
    meta[15] = 0

    count, texts = perm_ref.shape[1], slot_ref.shape[1]
    text = lax.broadcasted_iota(jnp.int32, (1, texts), 1)
    member = text & 7
    device = spot(x, y, z, core, text >> 3)
    tower = jnp.where(member < 6, device * 6 + member, -1)
    hit = lax.broadcasted_iota(jnp.int32, (count, texts), 0) == tower
    perm = perm_ref[...]
    high, low = (perm >> 5).astype(jnp.float32), (perm & 31).astype(jnp.float32)
    line = lax.broadcasted_iota(jnp.int32, (16, count), 0)
    digits = jnp.where(line == 0, high, jnp.where(line == 1, low, 0.0)).astype(jnp.bfloat16)
    found = jnp.dot(digits, hit.astype(jnp.bfloat16), preferred_element_type=jnp.float32)
    slot = (found[0:1] * 32.0 + found[1:2]).astype(jnp.int32)
    slot_ref[...] = jnp.where(tower >= 0, slot, -1)
    graph = lax.broadcasted_iota(jnp.int32, gid_ref.shape, 0)
    gid_ref[...] = spot(x, y, z, core, graph & 127) * 6 + (graph >> 7)

    own = graph_ref[...]
    norm = jnp.sqrt(jnp.sum(own * own, axis=-1, keepdims=True) + epsilon)
    unit = (own / norm).astype(jnp.bfloat16)
    take = lax.broadcasted_iota(jnp.int32, (16, own.shape[0]), 0) + col * 6
    take = take == lax.broadcasted_iota(jnp.int32, (16, own.shape[0]), 1)
    share = jnp.dot(take.astype(jnp.bfloat16), unit, preferred_element_type=jnp.float32)
    first = jnp.concatenate([share[k : k + 1] for k in range(4)], axis=1)
    second = jnp.concatenate([share[k : k + 1] for k in (4, 5)] * 2, axis=1)
    at = lax.broadcasted_iota(jnp.int32, rows_ref.shape, 0)
    rows_ref[...] = jnp.where(at == 6, first, jnp.where(at == 7, second, 0.0)).astype(jnp.bfloat16)


def prepare(text_hidden, lengths, perm, graph_emb):
    seqs, seq_len, width = text_hidden.shape
    count = perm.shape[0]
    smem, vmem = pl.BlockSpec(memory_space=pltpu.SMEM), pl.BlockSpec(memory_space=pltpu.VMEM)
    return pl.pallas_call(
        prepare_kernel,
        in_specs=[smem, pl.BlockSpec(memory_space=pl.ANY), vmem, vmem],
        out_specs=[smem, smem, vmem, vmem, vmem, vmem],
        out_shape=[
            jax.ShapeDtypeStruct((16,), jnp.int32),
            jax.ShapeDtypeStruct((2,), jnp.int32),
            jax.ShapeDtypeStruct((seqs * seq_len, width), jnp.bfloat16),
            jax.ShapeDtypeStruct((1, count // 6 * 8), jnp.int32),
            jax.ShapeDtypeStruct((count, 1), jnp.int32),
            jax.ShapeDtypeStruct((8, width), jnp.bfloat16),
        ],
        scratch_shapes=[pltpu.SemaphoreType.DMA],
        compiler_params=pltpu.CompilerParams(vmem_limit_bytes=12 * 2**20),
    )(lengths, text_hidden, perm.reshape(1, count), graph_emb)


def merge_bias(tiles, run, at=0):
    lane = lax.broadcasted_iota(jnp.int32, (1, tiles[0].shape[1]), 1) // run % 4
    row = tiles[0].astype(jnp.float32)[at : at + 1]
    for k in range(1, 4):
        row = jnp.where(lane == k, tiles[k].astype(jnp.float32)[at : at + 1], row)
    return jnp.broadcast_to(row, tiles[0].shape).astype(jnp.bfloat16)


def split_kernel(*refs):
    parts = refs[:4]
    for k, out in enumerate(refs[-2:]):
        for s, part in enumerate(parts):
            out[16 * s : 16 * s + 16, :] = part[16 * k : 16 * k + 16, :]
            out[64 + 16 * s : 80 + 16 * s, :] = part[32 + 16 * k : 48 + 16 * k, :]
        out[128:144, :] = merge_bias([p[64:80, :] for p in parts], 16, 8 * k)


def join_kernel(*refs):
    for k, out in enumerate(refs[-2:]):
        parts = refs[4 * k : 4 * k + 4]
        for s, part in enumerate(parts):
            out[64 * s : 64 * s + 64, :] = part[0:64, :]
            out[256 + 64 * s : 320 + 64 * s, :] = part[64:128, :]
        out[512:528, :] = merge_bias([p[128:144, :] for p in parts], 64)


def arrange(body, parts, rows, done=()):
    shape = jax.ShapeDtypeStruct((rows, parts[0].shape[1]), jnp.bfloat16)
    return pl.pallas_call(
        body,
        in_specs=[pl.BlockSpec(memory_space=pltpu.VMEM)] * len(parts)
        + [pl.BlockSpec(memory_space=pl.ANY)] * len(done),
        out_specs=[pl.BlockSpec(memory_space=pltpu.VMEM)] * 2,
        out_shape=[shape, shape],
        compiler_params=pltpu.CompilerParams(vmem_limit_bytes=4 * 2**20),
    )(*parts, *done)


def ffn_tiles(x, weights):
    up = jnp.concatenate([w[0:256, :] for w in weights], axis=0)
    down = jnp.concatenate([w[256:512, :] for w in weights], axis=0)
    bias = jnp.concatenate(
        [w[512:528, 0:256].astype(jnp.float32)[0:1] for w in weights], axis=1
    )
    rows = x.shape[0]
    halves = [x] if rows == block_rows else [x[: rows // 2], x[rows // 2 :]]
    preact = [
        lax.dot_general(h, up, nt, preferred_element_type=jnp.float32) + bias for h in halves
    ]
    parts = [
        jnp.dot(gelu_exact(p).astype(jnp.bfloat16), down, preferred_element_type=jnp.float32)
        for p in preact
    ]
    return jnp.concatenate(parts, axis=0)


def ffn_kernel(count, first, last, meta, x_ref, *refs):
    weights, refs = refs[:count], refs[count:]
    if not first:
        acc_in, refs = refs[0], refs[1:]
    if last:
        gain_ref, graph_ref, pooled_ref, sums = refs
        sums[...] = jnp.zeros_like(sums)
    else:
        out_ref, token_ref = refs
        token_ref[...] = jnp.zeros_like(token_ref)

    def rows_step(base, height):
        at = pl.ds(pl.multiple_of(base, block_rows), height)
        x = x_ref[at, :]
        total = ffn_tiles(x, weights)
        if not first:
            total = acc_in[at, :] + total
        if not last:
            out_ref[at, :] = total
            return
        summed = x.astype(jnp.float32) + total
        centre = summed - jnp.mean(summed, axis=-1, keepdims=True)
        spread = jnp.mean(centre * centre, axis=-1, keepdims=True)
        normed = centre * lax.rsqrt(spread + epsilon)
        row = base + lax.broadcasted_iota(jnp.int32, (height, 1), 0)
        groups = height // 16
        group = base + 16 * lax.broadcasted_iota(jnp.int32, (8, groups), 1)
        seq = lax.broadcasted_iota(jnp.int32, (8, groups), 0)
        valid = row < 0
        member = group < 0
        for s in range(6):
            start, stop = meta[s], meta[s] + meta[6 + s]
            valid |= (row >= start) & (row < stop)
            member |= (group >= start) & (group < stop) & (seq == s)
        normed = jnp.where(valid, normed, 0.0)
        partial = jnp.sum(normed.reshape(groups, 16, normed.shape[1]), axis=1)
        sums[...] += jnp.dot(
            member.astype(jnp.float32),
            partial,
            precision=lax.Precision.HIGHEST,
            preferred_element_type=jnp.float32,
        )

    blocks = meta[13]
    double = 2 * block_rows

    @pl.loop(0, blocks // 2)
    def _(i):
        rows_step(i * double, double)

    @pl.when(blocks % 2 == 1)
    def _():
        rows_step((blocks - 1) * block_rows, block_rows)

    if last:
        seq = lax.broadcasted_iota(jnp.int32, (8, 1), 0)
        tokens = jnp.ones((8, 1), jnp.float32)
        for s in range(6):
            tokens = jnp.where(seq == s, meta[6 + s].astype(jnp.float32), tokens)
        means = (sums[...] * gain_ref[...] / tokens).astype(jnp.bfloat16)
        pooled_ref[...] = jnp.where(seq < 6, means, graph_ref[...])


def ffn_step(meta, packed, weights, acc=None, gain=None, graph_rows=None):
    rows, width = packed.shape
    count, first, last = len(weights), acc is None, gain is not None
    operands = [packed, *weights]
    aliases = {}
    if not first:
        if not last:
            aliases = {1 + len(operands): 0}
        operands.append(acc)
    scratch = []
    if last:
        operands += [gain, graph_rows]
        out_shape = jax.ShapeDtypeStruct((8, width), jnp.bfloat16)
        scratch = [pltpu.VMEM((8, width), jnp.float32)]
    else:
        out_shape = [jax.ShapeDtypeStruct((rows, width), jnp.float32)]
        out_shape.append(jax.ShapeDtypeStruct((8, 128), jnp.float32))
    vmem = pl.BlockSpec(memory_space=pltpu.VMEM)
    return pl.pallas_call(
        functools.partial(ffn_kernel, count, first, last),
        in_specs=[pl.BlockSpec(memory_space=pltpu.SMEM)]
        + [pl.BlockSpec(memory_space=pltpu.VMEM)] * len(operands),
        out_specs=vmem if last else [vmem, vmem],
        scratch_shapes=scratch,
        out_shape=out_shape,
        input_output_aliases=aliases,
        compiler_params=pltpu.CompilerParams(vmem_limit_bytes=8 * 2**20),
        cost_estimate=pl.CostEstimate(
            flops=4 * rows * 256 * count * width, bytes_accessed=2**20, transcendentals=0
        ),
    )(meta, *operands)


def tie_kernel(*refs):
    del refs


def after(values, done):
    return pl.pallas_call(
        tie_kernel,
        in_specs=[pl.BlockSpec(memory_space=pl.ANY)] * (len(values) + 1),
        out_specs=[pl.BlockSpec(memory_space=pl.ANY)] * len(values),
        out_shape=[jax.ShapeDtypeStruct(v.shape, v.dtype) for v in values],
        input_output_aliases={k: k for k in range(len(values))},
        compiler_params=pltpu.CompilerParams(vmem_limit_bytes=2**20),
    )(*values, done)


def tail_kernel(place, *refs):
    pieces, refs = refs[:8], refs[8:]
    proj_ref, own_ref, slot_ref, gid_ref = refs[:4]
    loss_ref, grad_graph_ref, grad_text_ref, grad_proj_ref = refs[4:]
    flat, row_first = place[0], place[1]
    pooled = jnp.concatenate([p[...] for p in pieces], axis=0)
    texts = pooled.shape[0]
    graphs = gid_ref.shape[0]
    devices = texts // 8
    text_emb = jnp.dot(pooled, proj_ref[...], preferred_element_type=jnp.float32)
    text_norm = jnp.sqrt(jnp.sum(text_emb * text_emb, axis=-1, keepdims=True) + epsilon)
    text_unit = text_emb / text_norm
    text_send = text_unit.astype(jnp.bfloat16)
    line = lax.broadcasted_iota(jnp.int32, (2 * devices, texts), 0)
    wanted = jnp.where(line < devices, 8 * line + 6, 8 * (line - devices) + 7)
    carried = wanted == lax.broadcasted_iota(jnp.int32, (2 * devices, texts), 1)
    carriers = jnp.dot(
        carried.astype(jnp.bfloat16), pooled, preferred_element_type=jnp.float32
    ).astype(jnp.bfloat16)
    graph_send = jnp.concatenate(
        [carriers[0:devices, 256 * k : 256 * k + 256] for k in range(4)]
        + [carriers[devices:, 256 * k : 256 * k + 256] for k in range(2)],
        axis=0,
    )
    slot = slot_ref[...]
    valid = slot >= 0

    def scores(rows_send):
        logits = (
            lax.dot_general(rows_send, text_send, nt, preferred_element_type=jnp.float32)
            * sharpness
        )
        expo = jnp.where(valid, jnp.exp(logits), 0.0)
        return logits, expo, jnp.sum(expo, axis=1, keepdims=True)

    logits, expo, row_total = scores(graph_send)
    col_total = jnp.where(valid, jnp.sum(expo, axis=0, keepdims=True), 1.0)
    col_scale = 0.5 / col_total
    matched = gid_ref[...] == slot
    diagonal = jnp.sum(jnp.where(matched, logits, 0.0), axis=1, keepdims=True)
    row_terms = jnp.sum(jnp.log(row_total) - 2.0 * diagonal, axis=0, keepdims=True)
    col_terms = jnp.sum(jnp.log(col_total), axis=1, keepdims=True)
    loss_ref[...] = (row_terms + col_terms) / (2.0 * graphs)

    def weigh(expo, row_total, matched):
        weights = expo * (0.5 / row_total + col_scale)
        return (weights - jnp.where(matched, 1.0, 0.0)).astype(jnp.bfloat16)

    weights = weigh(expo, row_total, matched)
    text_grad = (
        lax.dot_general(weights, graph_send, tn, preferred_element_type=jnp.float32)
        * sharpness
    )
    along = jnp.sum(text_unit * text_grad, axis=-1, keepdims=True)
    grad_text = (text_grad - text_unit * along) / text_norm
    grad_text_ref[...] = grad_text[0:8]

    own = own_ref[...]
    own_norm = jnp.sqrt(jnp.sum(own * own, axis=-1, keepdims=True) + epsilon)
    own_unit = own / own_norm
    _, own_expo, own_total = scores(own_unit.astype(jnp.bfloat16))
    own_rows = own.shape[0]
    own_matched = row_first + lax.broadcasted_iota(jnp.int32, (own_rows, texts), 0) == slot
    own_weights = weigh(own_expo, own_total, own_matched)
    graph_grad = (
        jnp.dot(own_weights, text_send, preferred_element_type=jnp.float32) * sharpness
    )
    own_along = jnp.sum(own_unit * graph_grad, axis=-1, keepdims=True)
    grad_graph_ref[...] = (graph_grad - own_unit * own_along) / own_norm

    width = pooled.shape[1]
    feature = lax.broadcasted_iota(jnp.int32, (width, 128), 0)
    wanted = flat * 8 + lax.broadcasted_iota(jnp.int32, (width, 128), 1)
    pick = (feature == wanted).astype(jnp.bfloat16)
    picked = jnp.dot(pooled, pick, preferred_element_type=jnp.float32)
    grad_proj = lax.dot_general(
        picked,
        grad_text,
        tn,
        precision=lax.Precision.HIGHEST,
        preferred_element_type=jnp.float32,
    )
    grad_proj_ref[...] = grad_proj[0:8]


def tail(place, pieces, proj_weight, graph_emb, slot, gid):
    shapes = [(1, 1), graph_emb.shape, (8, 256), (8, 256)]
    return pl.pallas_call(
        tail_kernel,
        in_specs=[pl.BlockSpec(memory_space=pltpu.SMEM)]
        + [pl.BlockSpec(memory_space=pltpu.VMEM)] * 12,
        out_specs=[pl.BlockSpec(memory_space=pltpu.VMEM)] * 4,
        out_shape=[jax.ShapeDtypeStruct(s, jnp.float32) for s in shapes],
        compiler_params=pltpu.CompilerParams(vmem_limit_bytes=48 * 2**20),
    )(place, *pieces, proj_weight, graph_emb, slot, gid)


def gather_weights(up_weight, up_bias, down_weight, done):
    width = up_weight.shape[1]
    bias = [jnp.tile(b.reshape(1, 16), (8, width // 16)) for b in (up_bias[:16], up_bias[16:])]
    own = jnp.concatenate([up_weight, down_weight, *bias], axis=0)
    halves = arrange(split_kernel, from_line(own, "dz"), 144)
    pieces = []
    for half, inner in zip(halves, ("dx", "dy")):
        ahead, behind = (send(half, by_core=True, **{inner: hop}) for hop in (1, 3))
        pieces += [half, ahead, send(ahead, by_core=True, **{inner: 1}), behind]
    return arrange(join_kernel, pieces, 528, (done,))


def shards(
    text_hidden, lengths, up_weight, up_bias, down_weight, ln_gain, proj_weight, graph_emb, perm
):
    meta, place, packed, slot, gid, graph_rows = prepare(text_hidden, lengths, perm, graph_emb)
    mine = gather_weights(up_weight, up_bias, down_weight, graph_rows)
    step = functools.partial(ffn_step, meta, packed)
    acc = None
    for turn in range(4):
        other = [send(block, dc=1) for block in mine]
        if turn < 3:
            coming = [
                send(block, by_core=True, **{outer: 1}) for block, outer in zip(mine, ("dy", "dx"))
            ]
        acc, _ = step(mine, acc)
        if turn < 3:
            acc, token = step(other, acc)
            mine = after(coming, token)
    pooled = step(other, acc, ln_gain.reshape(1, -1), graph_rows)
    for axis in ("dz", "dy"):
        pooled = jnp.concatenate(from_line(pooled, axis), axis=0)
    line = from_line(pooled, "dx")
    pieces = line + [send(value, dc=1) for value in line]

    loss, grad_graph, grad_text, grad_proj = tail(
        place, pieces, proj_weight, graph_emb, slot, gid
    )
    return (loss[0, 0], grad_graph, grad_text[:6], grad_proj)


def solution(mesh):
    return jax.shard_map(
        shards,
        mesh=mesh,
        in_specs=(
            P(("row", "col"), None, None),
            P(("row", "col")),
            P(("row", "col"), None),
            P(("row", "col")),
            P(("row", "col"), None),
            P(),
            P(),
            P("row", None),
            P(),
        ),
        out_specs=(P(), P("row", None), P(("row", "col"), None), P(("row", "col"), None)),
        check_vma=False,
    )
```

```python
import functools

import jax
import jax.numpy as jnp
from jax import lax
from jax.experimental import pallas as pl
from jax.experimental.pallas import tpu as pltpu
from jax.sharding import PartitionSpec as P

sharpness = 1.0 / 0.02
epsilon = 1e-06
axes = ("row", "col")
block_rows = 256
erf_terms = (
    -5.7109417639367166e-08,
    2.812487991832313e-06,
    -4.7398178139701486e-05,
    -5.735534068662673e-05,
    0.03636491671204567,
    0.7978729605674744,
)
nt = (((1,), (1,)), ((), ()))
tn = (((0,), (0,)), ((), ()))


def flat_index(x, y, z, core):
    return (z * 8 + (x % 2) * 4 + y) * 4 + (x // 2) * 2 + core


def pairs(dx=0, dy=0, dz=0, dc=0, by_core=False):
    found = []
    for x in range(4):
        for y in range(4):
            for z in range(4):
                for core in range(2):
                    sign = -1 if by_core and core else 1
                    target = flat_index(
                        (x + sign * dx) % 4, (y + sign * dy) % 4, (z + sign * dz) % 4, core ^ dc
                    )
                    found.append((flat_index(x, y, z, core), target))
    return found


def send(value, **hop):
    return lax.ppermute(value, axes, pairs(**hop))


def from_line(value, axis):
    return [value] + [send(value, **{axis: hop}) for hop in (1, 3, 2)]


def gelu_exact(x):
    square = jnp.minimum(x * x, 25.0)
    series = jnp.full_like(square, erf_terms[0])
    for term in erf_terms[1:]:
        series = series * square + term
    half = 0.5 * x
    return half + half * jnp.tanh(x * series)


def spot(x, y, z, core, order):
    def away(here, step):
        moved = jnp.where(step == 1, 3, jnp.where(step == 2, 1, jnp.where(step == 3, 2, 0)))
        return (here + moved) & 3

    x, y = away(x, (order >> 4) & 3), away(y, (order >> 2) & 3)
    z, core = away(z, order & 3), core ^ ((order >> 6) & 1)
    return (z * 8 + (x & 1) * 4 + y) * 4 + (x >> 1) * 2 + core


def prepare_kernel(
    lengths, tokens_ref, perm_ref, graph_ref, meta, place, packed, slot_ref, gid_ref, rows_ref, sem
):
    row, col = lax.axis_index("row"), lax.axis_index("col")
    z, y, core = row >> 3, row & 3, col & 1
    x = (col >> 1) * 2 + ((row >> 2) & 1)
    place[0] = row * 4 + col
    place[1] = row * graph_ref.shape[0]
    start = jnp.int32(0)
    for s in range(6):
        meta[s] = start
        meta[6 + s] = lengths[s]
        begin = pl.multiple_of(start, 16)
        copy = pltpu.make_async_copy(tokens_ref.at[s], packed.at[pl.ds(begin, 256)], sem)
        copy.start()
        copy.wait()
        start = start + ((lengths[s] + 15) >> 4 << 4)
    meta[12] = start
    meta[13] = (start + block_rows - 1) // block_rows
    meta[14] = 0
    meta[15] = 0

    count, texts = perm_ref.shape[1], slot_ref.shape[1]
    text = lax.broadcasted_iota(jnp.int32, (1, texts), 1)
    member = text & 7
    device = spot(x, y, z, core, text >> 3)
    tower = jnp.where(member < 6, device * 6 + member, -1)
    hit = lax.broadcasted_iota(jnp.int32, (count, texts), 0) == tower
    perm = perm_ref[...]
    high, low = (perm >> 5).astype(jnp.float32), (perm & 31).astype(jnp.float32)
    line = lax.broadcasted_iota(jnp.int32, (16, count), 0)
    digits = jnp.where(line == 0, high, jnp.where(line == 1, low, 0.0)).astype(jnp.bfloat16)
    found = jnp.dot(digits, hit.astype(jnp.bfloat16), preferred_element_type=jnp.float32)
    slot = (found[0:1] * 32.0 + found[1:2]).astype(jnp.int32)
    slot_ref[...] = jnp.where(tower >= 0, slot, -1)
    graph = lax.broadcasted_iota(jnp.int32, gid_ref.shape, 0)
    gid_ref[...] = spot(x, y, z, core, graph & 127) * 6 + (graph >> 7)

    own = graph_ref[...]
    norm = jnp.sqrt(jnp.sum(own * own, axis=-1, keepdims=True) + epsilon)
    unit = (own / norm).astype(jnp.bfloat16)
    take = lax.broadcasted_iota(jnp.int32, (16, own.shape[0]), 0) + col * 6
    take = take == lax.broadcasted_iota(jnp.int32, (16, own.shape[0]), 1)
    share = jnp.dot(take.astype(jnp.bfloat16), unit, preferred_element_type=jnp.float32)
    first = jnp.concatenate([share[k : k + 1] for k in range(4)], axis=1)
    second = jnp.concatenate([share[k : k + 1] for k in (4, 5)] * 2, axis=1)
    at = lax.broadcasted_iota(jnp.int32, rows_ref.shape, 0)
    rows_ref[...] = jnp.where(at == 6, first, jnp.where(at == 7, second, 0.0)).astype(jnp.bfloat16)


def prepare(text_hidden, lengths, perm, graph_emb):
    seqs, seq_len, width = text_hidden.shape
    count = perm.shape[0]
    smem, vmem = pl.BlockSpec(memory_space=pltpu.SMEM), pl.BlockSpec(memory_space=pltpu.VMEM)
    return pl.pallas_call(
        prepare_kernel,
        in_specs=[smem, pl.BlockSpec(memory_space=pl.ANY), vmem, vmem],
        out_specs=[smem, smem, vmem, vmem, vmem, vmem],
        out_shape=[
            jax.ShapeDtypeStruct((16,), jnp.int32),
            jax.ShapeDtypeStruct((2,), jnp.int32),
            jax.ShapeDtypeStruct((seqs * seq_len, width), jnp.bfloat16),
            jax.ShapeDtypeStruct((1, count // 6 * 8), jnp.int32),
            jax.ShapeDtypeStruct((count, 1), jnp.int32),
            jax.ShapeDtypeStruct((8, width), jnp.bfloat16),
        ],
        scratch_shapes=[pltpu.SemaphoreType.DMA],
        compiler_params=pltpu.CompilerParams(vmem_limit_bytes=12 * 2**20),
    )(lengths, text_hidden, perm.reshape(1, count), graph_emb)


def merge_bias(tiles, run, at=0):
    lane = lax.broadcasted_iota(jnp.int32, (1, tiles[0].shape[1]), 1) // run % 4
    row = tiles[0].astype(jnp.float32)[at : at + 1]
    for k in range(1, 4):
        row = jnp.where(lane == k, tiles[k].astype(jnp.float32)[at : at + 1], row)
    return jnp.broadcast_to(row, tiles[0].shape).astype(jnp.bfloat16)


def split_kernel(*refs):
    parts = refs[:4]
    for k, out in enumerate(refs[-2:]):
        for s, part in enumerate(parts):
            out[16 * s : 16 * s + 16, :] = part[16 * k : 16 * k + 16, :]
            out[64 + 16 * s : 80 + 16 * s, :] = part[32 + 16 * k : 48 + 16 * k, :]
        out[128:144, :] = merge_bias([p[64:80, :] for p in parts], 16, 8 * k)


def join_kernel(*refs):
    for k, out in enumerate(refs[-2:]):
        parts = refs[4 * k : 4 * k + 4]
        for s, part in enumerate(parts):
            out[64 * s : 64 * s + 64, :] = part[0:64, :]
            out[256 + 64 * s : 320 + 64 * s, :] = part[64:128, :]
        out[512:528, :] = merge_bias([p[128:144, :] for p in parts], 64)


def arrange(body, parts, rows, done=()):
    shape = jax.ShapeDtypeStruct((rows, parts[0].shape[1]), jnp.bfloat16)
    return pl.pallas_call(
        body,
        in_specs=[pl.BlockSpec(memory_space=pltpu.VMEM)] * len(parts)
        + [pl.BlockSpec(memory_space=pl.ANY)] * len(done),
        out_specs=[pl.BlockSpec(memory_space=pltpu.VMEM)] * 2,
        out_shape=[shape, shape],
        compiler_params=pltpu.CompilerParams(vmem_limit_bytes=4 * 2**20),
    )(*parts, *done)


def ffn_tiles(x, weights):
    up = jnp.concatenate([w[0:256, :] for w in weights], axis=0)
    down = jnp.concatenate([w[256:512, :] for w in weights], axis=0)
    bias = jnp.concatenate(
        [w[512:528, 0:256].astype(jnp.float32)[0:1] for w in weights], axis=1
    )
    rows = x.shape[0]
    halves = [x] if rows == block_rows else [x[: rows // 2], x[rows // 2 :]]
    preact = [
        lax.dot_general(h, up, nt, preferred_element_type=jnp.float32) + bias for h in halves
    ]
    parts = [
        jnp.dot(gelu_exact(p).astype(jnp.bfloat16), down, preferred_element_type=jnp.float32)
        for p in preact
    ]
    return jnp.concatenate(parts, axis=0)


def ffn_kernel(count, first, last, meta, x_ref, *refs):
    weights, refs = refs[:count], refs[count:]
    if not first:
        acc_in, refs = refs[0], refs[1:]
    if last:
        gain_ref, graph_ref, pooled_ref, sums = refs
        sums[...] = jnp.zeros_like(sums)
    else:
        out_ref, token_ref = refs
        token_ref[...] = jnp.zeros_like(token_ref)

    def rows_step(base, height):
        at = pl.ds(pl.multiple_of(base, block_rows), height)
        x = x_ref[at, :]
        total = ffn_tiles(x, weights)
        if not first:
            total = acc_in[at, :] + total
        if not last:
            out_ref[at, :] = total
            return
        summed = x.astype(jnp.float32) + total
        centre = summed - jnp.mean(summed, axis=-1, keepdims=True)
        spread = jnp.mean(centre * centre, axis=-1, keepdims=True)
        normed = centre * lax.rsqrt(spread + epsilon) * gain_ref[...]
        row = base + lax.broadcasted_iota(jnp.int32, (height, 1), 0)
        groups = height // 16
        group = base + 16 * lax.broadcasted_iota(jnp.int32, (8, groups), 1)
        seq = lax.broadcasted_iota(jnp.int32, (8, groups), 0)
        valid = row < 0
        member = group < 0
        for s in range(6):
            start, stop = meta[s], meta[s] + meta[6 + s]
            valid |= (row >= start) & (row < stop)
            member |= (group >= start) & (group < stop) & (seq == s)
        normed = jnp.where(valid, normed, 0.0)
        partial = jnp.sum(normed.reshape(groups, 16, normed.shape[1]), axis=1)
        sums[...] += jnp.dot(
            member.astype(jnp.float32),
            partial,
            precision=lax.Precision.HIGHEST,
            preferred_element_type=jnp.float32,
        )

    blocks = meta[13]
    double = 2 * block_rows

    @pl.loop(0, blocks // 2)
    def _(i):
        rows_step(i * double, double)

    @pl.when(blocks % 2 == 1)
    def _():
        rows_step((blocks - 1) * block_rows, block_rows)

    if last:
        seq = lax.broadcasted_iota(jnp.int32, (8, 1), 0)
        tokens = jnp.ones((8, 1), jnp.float32)
        for s in range(6):
            tokens = jnp.where(seq == s, meta[6 + s].astype(jnp.float32), tokens)
        means = (sums[...] / tokens).astype(jnp.bfloat16)
        pooled_ref[...] = jnp.where(seq < 6, means, graph_ref[...])


def ffn_step(meta, packed, weights, acc=None, gain=None, graph_rows=None):
    rows, width = packed.shape
    count, first, last = len(weights), acc is None, gain is not None
    operands = [packed, *weights]
    aliases = {}
    if not first:
        if not last:
            aliases = {1 + len(operands): 0}
        operands.append(acc)
    scratch = []
    if last:
        operands += [gain, graph_rows]
        out_shape = jax.ShapeDtypeStruct((8, width), jnp.bfloat16)
        scratch = [pltpu.VMEM((8, width), jnp.float32)]
    else:
        out_shape = [jax.ShapeDtypeStruct((rows, width), jnp.float32)]
        out_shape.append(jax.ShapeDtypeStruct((8, 128), jnp.float32))
    vmem = pl.BlockSpec(memory_space=pltpu.VMEM)
    return pl.pallas_call(
        functools.partial(ffn_kernel, count, first, last),
        in_specs=[pl.BlockSpec(memory_space=pltpu.SMEM)]
        + [pl.BlockSpec(memory_space=pltpu.VMEM)] * len(operands),
        out_specs=vmem if last else [vmem, vmem],
        scratch_shapes=scratch,
        out_shape=out_shape,
        input_output_aliases=aliases,
        compiler_params=pltpu.CompilerParams(vmem_limit_bytes=8 * 2**20),
        cost_estimate=pl.CostEstimate(
            flops=4 * rows * 256 * count * width, bytes_accessed=2**20, transcendentals=0
        ),
    )(meta, *operands)


def tie_kernel(*refs):
    del refs


def after(values, done):
    return pl.pallas_call(
        tie_kernel,
        in_specs=[pl.BlockSpec(memory_space=pl.ANY)] * (len(values) + 1),
        out_specs=[pl.BlockSpec(memory_space=pl.ANY)] * len(values),
        out_shape=[jax.ShapeDtypeStruct(v.shape, v.dtype) for v in values],
        input_output_aliases={k: k for k in range(len(values))},
        compiler_params=pltpu.CompilerParams(vmem_limit_bytes=2**20),
    )(*values, done)


def tail_kernel(place, *refs):
    pieces, refs = refs[:8], refs[8:]
    proj_ref, own_ref, slot_ref, gid_ref = refs[:4]
    loss_ref, grad_graph_ref, grad_text_ref, grad_proj_ref = refs[4:]
    flat, row_first = place[0], place[1]
    pooled = jnp.concatenate([p[...] for p in pieces], axis=0)
    texts = pooled.shape[0]
    graphs = gid_ref.shape[0]
    devices = texts // 8
    text_emb = jnp.dot(pooled, proj_ref[...], preferred_element_type=jnp.float32)
    text_norm = jnp.sqrt(jnp.sum(text_emb * text_emb, axis=-1, keepdims=True) + epsilon)
    text_unit = text_emb / text_norm
    text_send = text_unit.astype(jnp.bfloat16)
    line = lax.broadcasted_iota(jnp.int32, (2 * devices, texts), 0)
    wanted = jnp.where(line < devices, 8 * line + 6, 8 * (line - devices) + 7)
    carried = wanted == lax.broadcasted_iota(jnp.int32, (2 * devices, texts), 1)
    carriers = jnp.dot(
        carried.astype(jnp.bfloat16), pooled, preferred_element_type=jnp.float32
    ).astype(jnp.bfloat16)
    graph_send = jnp.concatenate(
        [carriers[0:devices, 256 * k : 256 * k + 256] for k in range(4)]
        + [carriers[devices:, 256 * k : 256 * k + 256] for k in range(2)],
        axis=0,
    )
    slot = slot_ref[...]
    valid = slot >= 0

    def scores(rows_send):
        logits = (
            lax.dot_general(rows_send, text_send, nt, preferred_element_type=jnp.float32)
            * sharpness
        )
        expo = jnp.where(valid, jnp.exp(logits), 0.0)
        return logits, expo, jnp.sum(expo, axis=1, keepdims=True)

    logits, expo, row_total = scores(graph_send)
    col_total = jnp.where(valid, jnp.sum(expo, axis=0, keepdims=True), 1.0)
    col_scale = 0.5 / col_total
    matched = gid_ref[...] == slot
    diagonal = jnp.sum(jnp.where(matched, logits, 0.0), axis=1, keepdims=True)
    row_terms = jnp.sum(jnp.log(row_total) - 2.0 * diagonal, axis=0, keepdims=True)
    col_terms = jnp.sum(jnp.log(col_total), axis=1, keepdims=True)
    loss_ref[...] = (row_terms + col_terms) / (2.0 * graphs)

    def weigh(expo, row_total, matched):
        weights = expo * (0.5 / row_total) + expo * col_scale
        return (weights - jnp.where(matched, 1.0, 0.0)).astype(jnp.bfloat16)

    weights = weigh(expo, row_total, matched)
    text_grad = (
        lax.dot_general(weights, graph_send, tn, preferred_element_type=jnp.float32)
        * sharpness
    )
    along = jnp.sum(text_unit * text_grad, axis=-1, keepdims=True)
    grad_text = (text_grad - text_unit * along) / text_norm
    grad_text_ref[...] = grad_text[0:8]

    own = own_ref[...]
    own_norm = jnp.sqrt(jnp.sum(own * own, axis=-1, keepdims=True) + epsilon)
    own_unit = own / own_norm
    _, own_expo, own_total = scores(own_unit.astype(jnp.bfloat16))
    own_rows = own.shape[0]
    own_matched = row_first + lax.broadcasted_iota(jnp.int32, (own_rows, texts), 0) == slot
    own_weights = weigh(own_expo, own_total, own_matched)
    graph_grad = (
        jnp.dot(own_weights, text_send, preferred_element_type=jnp.float32) * sharpness
    )
    own_along = jnp.sum(own_unit * graph_grad, axis=-1, keepdims=True)
    grad_graph_ref[...] = (graph_grad - own_unit * own_along) / own_norm

    width = pooled.shape[1]
    feature = lax.broadcasted_iota(jnp.int32, (width, 128), 0)
    wanted = flat * 8 + lax.broadcasted_iota(jnp.int32, (width, 128), 1)
    pick = (feature == wanted).astype(jnp.bfloat16)
    picked = jnp.dot(pooled, pick, preferred_element_type=jnp.float32)
    grad_proj = lax.dot_general(
        picked,
        grad_text,
        tn,
        precision=lax.Precision.HIGHEST,
        preferred_element_type=jnp.float32,
    )
    grad_proj_ref[...] = grad_proj[0:8]


def tail(place, pieces, proj_weight, graph_emb, slot, gid):
    shapes = [(1, 1), graph_emb.shape, (8, 256), (8, 256)]
    return pl.pallas_call(
        tail_kernel,
        in_specs=[pl.BlockSpec(memory_space=pltpu.SMEM)]
        + [pl.BlockSpec(memory_space=pltpu.VMEM)] * 12,
        out_specs=[pl.BlockSpec(memory_space=pltpu.VMEM)] * 4,
        out_shape=[jax.ShapeDtypeStruct(s, jnp.float32) for s in shapes],
        compiler_params=pltpu.CompilerParams(vmem_limit_bytes=48 * 2**20),
    )(place, *pieces, proj_weight, graph_emb, slot, gid)


def gather_weights(up_weight, up_bias, down_weight, done):
    width = up_weight.shape[1]
    bias = [jnp.tile(b.reshape(1, 16), (8, width // 16)) for b in (up_bias[:16], up_bias[16:])]
    own = jnp.concatenate([up_weight, down_weight, *bias], axis=0)
    halves = arrange(split_kernel, from_line(own, "dz"), 144)
    pieces = []
    for half, inner in zip(halves, ("dx", "dy")):
        ahead, behind = (send(half, by_core=True, **{inner: hop}) for hop in (1, 3))
        pieces += [half, ahead, send(ahead, by_core=True, **{inner: 1}), behind]
    return arrange(join_kernel, pieces, 528, (done,))


def shards(
    text_hidden, lengths, up_weight, up_bias, down_weight, ln_gain, proj_weight, graph_emb, perm
):
    meta, place, packed, slot, gid, graph_rows = prepare(text_hidden, lengths, perm, graph_emb)
    mine = gather_weights(up_weight, up_bias, down_weight, graph_rows)
    step = functools.partial(ffn_step, meta, packed)
    onward = lambda pair, hop: [
        send(block, by_core=True, **{outer: hop}) for block, outer in zip(pair, ("dy", "dx"))
    ]
    across = lambda pair: [send(block, dc=1) for block in pair]

    ahead, behind = onward(mine, 1), onward(mine, 3)
    other = across(mine)
    acc, _ = step(mine)
    acc, token = step(other, acc)
    tied = after([*ahead, *behind], token)

    ahead, behind = tied[:2], tied[2:]
    far = onward(ahead, 1)
    other_ahead, other_behind = across(ahead), across(behind)
    acc, _ = step(ahead, acc)
    acc, _ = step(behind, acc)
    acc, _ = step(other_ahead, acc)
    acc, token = step(other_behind, acc)
    far = after(far, token)

    other = across(far)
    acc, _ = step(far, acc)
    pooled = step(other, acc, ln_gain.reshape(1, -1), graph_rows)
    for axis in ("dz", "dy"):
        pooled = jnp.concatenate(from_line(pooled, axis), axis=0)
    line = from_line(pooled, "dx")
    pieces = line + [send(value, dc=1) for value in line]

    loss, grad_graph, grad_text, grad_proj = tail(
        place, pieces, proj_weight, graph_emb, slot, gid
    )
    return (loss[0, 0], grad_graph, grad_text[:6], grad_proj)


def solution(mesh):
    return jax.shard_map(
        shards,
        mesh=mesh,
        in_specs=(
            P(("row", "col"), None, None),
            P(("row", "col")),
            P(("row", "col"), None),
            P(("row", "col")),
            P(("row", "col"), None),
            P(),
            P(),
            P("row", None),
            P(),
        ),
        out_specs=(P(), P("row", None), P(("row", "col"), None), P(("row", "col"), None)),
        check_vma=False,
    )
```
